32 devices in a mesh: batch: 4 (over y, x), expert: 8 (over z, core).
Axes of the slice: x: 2, y: 2, z: 4, core: 2. Of those that a mesh axis runs over, the one named last changes fastest.
Arguments:
- tokens: bfloat16 [256, 4096], P(('batch', 'expert')), may hold values from -6 to 6
- expert_ids: int32 [256, 8], P(('batch', 'expert')), may hold values from 0 to 15, all different within a row; in each aligned block of 8 rows (0 to 7, 8 to 15, ...) at most 8 rows name the same one
- route_weights: float32 [256, 8], P(('batch', 'expert')), may hold values from 0.1 to 1
- in_weights: bfloat16 [16, 1536, 2, 4096], P('expert', 'batch'), may hold values from -0.09375 to 0.09375
- out_weights: bfloat16 [16, 1536, 4096], P('expert', 'batch'), may hold values from -0.15625 to 0.15625
Outputs:
- combined: bfloat16 [256, 4096], P(('batch', 'expert'))
The draws below stay inside these ranges and needn't reach their ends.
Inputs may be any that keep to these rules, and one draw needn't show every extreme that they name: `expert_ids`: each row names 8 different experts. Among the 8 rows of one device no expert is named more than 8 times, a bound that some block reaches.
All inputs are finite; a program needn't handle non-finite values.
Results may differ from the reference program's by a relative error of at most 0.0057.
Values may be sent and summed in bfloat16 or wider, within the bound.
No kernel may reach another device: no remote copies, remote signals or barrier semaphores. Data moves between devices by JAX's collectives and lax.ppermute only.
A program may use at most 192 MiB of HBM per device.

```python
import math
import jax
import jax.numpy as jnp
import numpy as np
from jax import lax

D = 4096
FF = 1536
TOP = 8
TOK_DEV = 8
EXPERTS = 16
TOKENS = 256
MOST = 8


def shard_levels(own_key, dims, split, smallest, high):
    gain = 1.0
    for position, shards_of in split:
        heights = jax.random.uniform(jax.random.fold_in(jax.random.fold_in(own_key, 6), position), (shards_of,), jnp.float32, smallest / len(split), high / len(split))
        gain = gain * jnp.repeat(jnp.exp(heights), dims[position] // shards_of).reshape((-1,) + (1,) * (len(dims) - 1 - position))
    return gain


def shared_out(own_key, own, number, rows, count, top, bound, lean):
    sequence = jax.random.permutation(own_key, count)
    crowded, usual = load_shares(count, rows * top, bound, lean, True), load_shares(count, rows * top, bound, lean, False)
    places = jnp.arange(count)

    def named(lengths, rotation):
        used = int((lengths > 0).sum())
        fixed = max(1, used // 4)
        moved = fixed + (places - fixed + rotation * (used - fixed)) % max(1, count - fixed)
        return jnp.zeros((count,), jnp.int32).at[sequence[jnp.where(places < fixed, places, moved)]].set(jnp.asarray(lengths, jnp.int32))

    lengths = jnp.where(number % 4 == 0, named(crowded, number // 4), named(usual, number - number // 4 - 1))
    mixed = jax.random.permutation(jax.random.fold_in(own, 3), count)
    source_of, sink = mixed[0:count // 2 * 2:2], mixed[1:count // 2 * 2:2]
    margin = jnp.minimum(lengths[source_of] - 1, bound - lengths[sink]) // 2
    margin = jnp.where((source_of == sequence[0]) | (sink == sequence[0]) | (lengths[sink] == 0), 0, jnp.maximum(margin, 0))
    moved = jax.random.randint(jax.random.fold_in(own, 4), (count // 2,), 0, 1 << 20) % (margin + 1)
    lengths = lengths.at[source_of].add(-moved).at[sink].add(moved)
    labels = jnp.searchsorted(jnp.cumsum(lengths), jnp.arange(rows * top), side="right").astype(jnp.int32)
    grid = labels.reshape(top, rows).T
    grid = grid[jax.random.permutation(jax.random.fold_in(own, 1), rows)]
    rotation = jax.random.randint(jax.random.fold_in(own, 2), (rows, 1), 0, top)
    return jnp.take_along_axis(grid, (jnp.arange(top)[None, :] + rotation) % top, axis=1)


def load_shares(count, total, most, slope, full):
    loads = [(1 << 20) // math.isqrt(standing ** slope) + 1 for standing in range(1, count + 1)]
    largest = most if full else min(most, max(-(-total // count), total * loads[0] // sum(loads)))
    least = 1 if total - largest >= count - 1 else 0
    counts, spare = [largest] + [least] * (count - 1), total - largest - least * (count - 1)
    while spare > 0:
        free = [i for i in range(1, count) if counts[i] < largest] or [i for i in range(1, count) if counts[i] < most]
        pool, left = sum([loads[i] for i in free]), spare
        for i in free:
            extra = min(most - counts[i], max(1, left * loads[i] // pool), spare)
            counts[i] = counts[i] + extra
            spare = spare - extra
    return np.array(counts)


def normal_values(own_key, dims, deviation, bound, pieces=(), kind=jnp.bfloat16):
    level = shard_levels(own_key, dims, pieces, -0.22, 0.18) if pieces else 1.0
    values = jax.random.normal(own_key, dims, jnp.float32) * deviation * level
    return jnp.minimum(jnp.maximum(values, -bound), bound).astype(kind)


def setup_inputs(seed: int = 0) -> dict:
    arg_keys = jax.random.split(jax.random.key(seed), 6)
    tokens = normal_values(arg_keys[0], (TOKENS, D), 1.0, 6.0, ((0, 32),))
    expert_ids_keys = jax.random.split(jax.random.fold_in(arg_keys[1], 1), TOKENS // TOK_DEV)
    expert_ids_turns = jax.random.permutation(jax.random.fold_in(arg_keys[1], 3), TOKENS // TOK_DEV)
    expert_ids = jax.vmap(lambda own, number: shared_out(jax.random.fold_in(arg_keys[1], 2), own, number, TOK_DEV, EXPERTS, TOP, MOST, 1))(expert_ids_keys, expert_ids_turns).reshape((TOKENS, TOP))
    route_weights = jnp.clip(jnp.exp(math.log(1.0) - 2.3025851 * jax.random.uniform(arg_keys[2], (TOKENS, TOP), jnp.float32) ** shard_levels(arg_keys[2], (TOKENS, TOP), ((0, 32),), -0.2, 0.2)), 0.1, 1.0)
    in_weights = normal_values(arg_keys[3], (EXPERTS, FF, 2, D), D ** -0.5, 0.09375, ((0, 8), (1, 4)))
    out_weights = normal_values(arg_keys[4], (EXPERTS, FF, D), FF ** -0.5, 0.15625, ((0, 8), (1, 4)))
    return dict(tokens=tokens, expert_ids=expert_ids, route_weights=route_weights, in_weights=in_weights, out_weights=out_weights)


def expert_rows(row_block, w_in, w_out):
    gate = jnp.dot(row_block, w_in[:, 0, :].T, preferred_element_type=jnp.float32)
    upper = jnp.dot(row_block, w_in[:, 1, :].T, preferred_element_type=jnp.float32)
    hidden = (jax.nn.silu(gate) * upper).astype(jnp.bfloat16)
    return jnp.dot(hidden, w_out, preferred_element_type=jnp.float32).astype(jnp.bfloat16)


def reference(tokens, expert_ids, route_weights, in_weights, out_weights):
    flat_ids = expert_ids.reshape(-1).astype(jnp.int32)
    flat_weights = route_weights.reshape(-1)
    capacity = (TOKENS // TOK_DEV) * MOST

    def visit(running, expert_index):
        chosen = flat_ids == expert_index
        hits = jnp.nonzero(chosen, size=capacity, fill_value=0)[0].astype(jnp.int32)
        valid = jnp.arange(capacity) < jnp.sum(chosen)
        token_index = hits // TOP
        produced = expert_rows(tokens[token_index], in_weights[expert_index], out_weights[expert_index])
        scaled = jnp.where(valid, flat_weights[hits], 0.0)
        running = running.at[token_index].add(scaled[:, None] * produced.astype(running.dtype))
        return running, None

    running, _ = lax.scan(visit, jnp.zeros((TOKENS, D), jnp.float32), jnp.arange(EXPERTS, dtype=jnp.int32))
    return running.astype(jnp.bfloat16)
```

```python
import functools

import jax
import jax.numpy as jnp
from jax import lax
from jax.experimental import pallas as pl
from jax.experimental.pallas import tpu as pltpu
from jax.sharding import PartitionSpec as P

LANES = 128
MIB = 1 << 20


def swap(block, axis, flips):
    size = lax.axis_size(axis)
    return lax.ppermute(block, axis, [(i, i ^ flips) for i in range(size)])


def gather_over(block, axis, steps):
    return jnp.concatenate([block] + [swap(block, axis, step) for step in steps], axis=0)


def packed_weights(expert_ids, route_weights, experts, width):
    onehot = expert_ids[:, :, None] == jnp.arange(experts, dtype=jnp.int32)
    dense = jnp.sum(jnp.where(onehot, route_weights[:, :, None], 0.0), axis=1)
    parts = []
    for _ in range(3):
        part = dense.astype(jnp.bfloat16)
        parts.append(part)
        dense = dense - part.astype(jnp.float32)
    packed = jnp.concatenate(parts, axis=1)
    return jnp.pad(packed, ((0, 0), (0, width - packed.shape[1])))


def load_kernel(in_ref, out_ref, in_vmem, out_vmem, sems):
    tiles = in_vmem.shape[0]
    copies = []
    for t in range(tiles):
        copies.append(
            pltpu.make_async_copy(
                in_ref.at[:, :, pl.ds(t * LANES, LANES)], in_vmem.at[t], sems.at[t]
            )
        )
    copies.append(pltpu.make_async_copy(out_ref, out_vmem, sems.at[tiles]))
    for copy in copies:
        copy.start()
    for copy in copies:
        copy.wait()


def load_weights(w_in, w_out):
    units, _, width = w_in.shape
    tiles = width // LANES
    return pl.pallas_call(
        load_kernel,
        out_shape=(
            pltpu.VMEM((tiles, units, 2, LANES), w_in.dtype),
            pltpu.VMEM(w_out.shape, w_out.dtype),
        ),
        in_specs=[pl.BlockSpec(memory_space=pltpu.HBM)] * 2,
        out_specs=[pl.BlockSpec(memory_space=pltpu.VMEM)] * 2,
        scratch_shapes=[pltpu.SemaphoreType.DMA((tiles + 1,))],
        compiler_params=pltpu.CompilerParams(vmem_limit_bytes=2 * MIB),
        cost_estimate=pl.CostEstimate(
            flops=0, bytes_accessed=2 * (w_in.size + w_out.size), transcendentals=0
        ),
    )(*(pltpu.with_memory_space_constraint(w, pltpu.HBM) for w in (w_in, w_out)))


def expert_kernel(exp_dev, select_ref, x_ref, win_ref, wout_ref, send_ref, keep_ref, mixed, hidden):
    halves, half_rows, _ = x_ref.shape
    rows = halves * half_rows
    tiles, lines, _ = win_ref.shape
    width = tiles * LANES
    per = lines // exp_dev
    x = x_ref[:, :, :width].reshape(rows, width)
    tail = x_ref[:, :, width:].reshape(rows, x_ref.shape[2] - width)
    contract_last = (((1,), (1,)), ((), ()))
    scale = lax.dot_general(
        select_ref[...], tail, contract_last, preferred_element_type=jnp.float32
    )
    for e in range(exp_dev):
        w = jnp.concatenate([win_ref[t, pl.ds(e * per, per), :] for t in range(tiles)], axis=1)
        both = lax.dot_general(w, x, contract_last, preferred_element_type=jnp.float32)
        for r in range(0, rows, LANES):
            mixed[...] = both[:, r : r + LANES]
            gate = mixed[pl.ds(0, per // 2, stride=2), :]
            up = mixed[pl.ds(1, per // 2, stride=2), :]
            act = gate / (1.0 + jnp.exp(-gate)) * up * scale[e : e + 1, r : r + LANES]
            hidden[pl.ds(e * per // 2, per // 2), r : r + LANES] = act.astype(jnp.bfloat16)
    chunk = min(512, width)
    for c in range(0, width, chunk):
        part = lax.dot_general(
            hidden[...],
            wout_ref[:, c : c + chunk],
            (((0,), (0,)), ((), ())),
            preferred_element_type=jnp.float32,
        )
        keep_ref[:, c : c + chunk] = part[:half_rows]
        send_ref[:, c : c + chunk] = part[half_rows:].astype(jnp.bfloat16)


def run_experts(select, x, win, wout, exp_dev):
    halves, half_rows, packed_width = x.shape
    tiles, lines, _ = win.shape
    width = tiles * LANES
    block = min(half_rows, 128)
    return pl.pallas_call(
        functools.partial(expert_kernel, exp_dev),
        grid=(half_rows // block,),
        out_shape=(
            jax.ShapeDtypeStruct((half_rows, width), jnp.bfloat16),
            jax.ShapeDtypeStruct((half_rows, width), jnp.float32),
        ),
        in_specs=[
            pl.BlockSpec(select.shape, lambda i: (0, 0)),
            pl.BlockSpec((halves, block, packed_width), lambda i: (0, i, 0)),
            pl.BlockSpec(memory_space=pltpu.VMEM),
            pl.BlockSpec(memory_space=pltpu.VMEM),
        ],
        out_specs=[
            pl.BlockSpec((block, width), lambda i: (i, 0)),
            pl.BlockSpec((block, width), lambda i: (i, 0)),
        ],
        scratch_shapes=[
            pltpu.VMEM((lines // exp_dev, LANES), jnp.float32),
            pltpu.VMEM((lines // 2, halves * block), jnp.bfloat16),
        ],
        compiler_params=pltpu.CompilerParams(vmem_limit_bytes=16 * MIB),
        cost_estimate=pl.CostEstimate(
            flops=3 * halves * half_rows * width * lines,
            bytes_accessed=2 * x.size + 6 * half_rows * width,
            transcendentals=halves * half_rows * lines // 2,
        ),
    )(select, x, win, wout)


def body(tokens, expert_ids, route_weights, in_weights, out_weights):
    tok_dev, width = tokens.shape
    exp_dev, units = in_weights.shape[:2]
    groups = lax.axis_size("expert")
    planes = lax.axis_size("batch")
    chips = groups // 2
    experts = exp_dev * groups
    tail = -(-3 * experts // LANES) * LANES

    win, wout = load_weights(
        in_weights.reshape(exp_dev * units, 2, width), out_weights.reshape(exp_dev * units, width)
    )
    win = win.reshape(width // LANES, exp_dev * units * 2, LANES)

    packed = packed_weights(expert_ids, route_weights, experts, tail)
    x = jnp.concatenate([tokens, packed], axis=1)
    x = gather_over(x, "expert", [2 * i for i in range(1, chips)])
    x = gather_over(x, "batch", range(1, planes))
    half_rows = x.shape[0]
    x = gather_over(x, "expert", [1]).reshape(2, half_rows, width + tail)

    wanted = lax.axis_index("expert") * exp_dev + jnp.arange(exp_dev, dtype=jnp.int32)
    column = jnp.arange(tail, dtype=jnp.int32)
    select = (column[None, :] % experts == wanted[:, None]) & (column < 3 * experts)[None, :]
    select = jnp.pad(select.astype(jnp.bfloat16), ((0, -exp_dev % 16), (0, 0)))

    send, total = run_experts(select, x, win, wout, exp_dev)
    total = total + swap(send, "expert", 1).astype(jnp.float32)
    for axis, steps in (
        ("batch", list(range(1, planes))),
        ("expert", [2 * i for i in range(1, chips)]),
    ):
        size = total.shape[0] // (len(steps) + 1)
        pieces = [total[i * size : (i + 1) * size] for i in range(len(steps) + 1)]
        total = pieces[0]
        for i, step in enumerate(steps):
            total = total + swap(pieces[i + 1].astype(jnp.bfloat16), axis, step).astype(jnp.float32)
    return total.astype(jnp.bfloat16)


def solution(mesh):
    return jax.shard_map(
        body,
        mesh=mesh,
        in_specs=(
            P(("batch", "expert"), None),
            P(("batch", "expert"), None),
            P(("batch", "expert"), None),
            P("expert", "batch", None, None),
            P("expert", "batch", None),
        ),
        out_specs=P(("batch", "expert"), None),
        check_vma=False,
    )
```

```python
import functools

import jax
import jax.numpy as jnp
from jax import lax
from jax.experimental import pallas as pl
from jax.experimental.pallas import tpu as pltpu
from jax.sharding import PartitionSpec as P

LANES = 128
MIB = 1 << 20
VMEM = pl.BlockSpec(memory_space=pltpu.VMEM)


def swap(block, axis, flips):
    size = lax.axis_size(axis)
    return lax.ppermute(block, axis, [(i, i ^ flips) for i in range(size)])


def pack_kernel(experts, tokens_ref, ids_ref, weights_ref, packed_ref):
    rows, width = tokens_ref.shape
    tail = packed_ref.shape[1] - width
    packed_ref[:, :width] = tokens_ref[...]
    lane = lax.broadcasted_iota(jnp.int32, (rows, tail), 1)
    expert = lane % experts
    part = lane // experts
    dense = jnp.zeros((rows, tail), jnp.float32)
    for k in range(ids_ref.shape[1]):
        dense += jnp.where(ids_ref[:, k : k + 1] == expert, weights_ref[:, k : k + 1], 0.0)
    result = jnp.zeros((rows, tail), jnp.float32)
    for step in range(3):
        rounded = dense.astype(jnp.bfloat16).astype(jnp.float32)
        result = jnp.where(part == step, rounded, result)
        dense = dense - rounded
    packed_ref[:, width:] = result.astype(jnp.bfloat16)


def pack(tokens, expert_ids, route_weights, experts):
    rows, width = tokens.shape
    tail = -(-3 * experts // LANES) * LANES
    return pl.pallas_call(
        functools.partial(pack_kernel, experts),
        out_shape=jax.ShapeDtypeStruct((rows, width + tail), jnp.bfloat16),
        in_specs=[VMEM] * 3,
        out_specs=VMEM,
        compiler_params=pltpu.CompilerParams(vmem_limit_bytes=2 * MIB),
    )(tokens, expert_ids, route_weights)


def stack_kernel(*refs):
    out_ref = refs[-1]
    start = 0
    for ref in refs[:-1]:
        out_ref[start : start + ref.shape[0], :] = ref[...]
        start += ref.shape[0]


def stack(blocks):
    rows = sum(block.shape[0] for block in blocks)
    return pl.pallas_call(
        stack_kernel,
        out_shape=jax.ShapeDtypeStruct((rows, blocks[0].shape[1]), blocks[0].dtype),
        in_specs=[VMEM] * len(blocks),
        out_specs=VMEM,
        compiler_params=pltpu.CompilerParams(vmem_limit_bytes=4 * MIB),
    )(*blocks)


def load_kernel(in_ref, out_ref, in_vmem, out_vmem, sems):
    tiles = in_vmem.shape[0]
    copies = [
        pltpu.make_async_copy(in_ref.at[:, :, pl.ds(t * LANES, LANES)], in_vmem.at[t], sems.at[t])
        for t in range(tiles)
    ]
    copies.append(pltpu.make_async_copy(out_ref, out_vmem, sems.at[tiles]))
    for copy in copies:
        copy.start()
    for copy in copies:
        copy.wait()


def load_weights(w_in, w_out):
    units, _, width = w_in.shape
    tiles = width // LANES
    win, wout = pl.pallas_call(
        load_kernel,
        out_shape=(
            pltpu.VMEM((tiles, units, 2, LANES), w_in.dtype),
            pltpu.VMEM(w_out.shape, w_out.dtype),
        ),
        in_specs=[pl.BlockSpec(memory_space=pltpu.HBM)] * 2,
        out_specs=[VMEM] * 2,
        scratch_shapes=[pltpu.SemaphoreType.DMA((tiles + 1,))],
        compiler_params=pltpu.CompilerParams(vmem_limit_bytes=2 * MIB),
        cost_estimate=pl.CostEstimate(
            flops=0, bytes_accessed=4 * (w_in.size + w_out.size), transcendentals=0
        ),
    )(*(pltpu.with_memory_space_constraint(w, pltpu.HBM) for w in (w_in, w_out)))
    return win.reshape(tiles, units * 2, LANES), wout


def expert_kernel(exp_dev, half, *refs):
    select_ref = refs[0]
    x_refs = refs[1 : 1 + 2 * half]
    win_ref, wout_ref, send_ref, keep_ref, mixed, hidden = refs[1 + 2 * half :]
    lines = win_ref.shape[1]
    width = win_ref.shape[0] * LANES
    per = lines // exp_dev
    block = x_refs[0].shape[0]
    rows = 2 * half * block
    x = jnp.concatenate([ref[:, :width] for ref in x_refs], axis=0)
    tail = jnp.concatenate([ref[:, width:] for ref in x_refs], axis=0)
    contract_last = (((1,), (1,)), ((), ()))
    scale = lax.dot_general(
        select_ref[...], tail, contract_last, preferred_element_type=jnp.float32
    )
    for e in range(exp_dev):
        w = jnp.concatenate(
            [win_ref[t, pl.ds(e * per, per), :] for t in range(win_ref.shape[0])], axis=1
        )
        both = lax.dot_general(w, x, contract_last, preferred_element_type=jnp.float32)
        for r in range(0, rows, LANES):
            mixed[...] = both[:, r : r + LANES]
            gate = mixed[pl.ds(0, per // 2, stride=2), :]
            up = mixed[pl.ds(1, per // 2, stride=2), :]
            act = gate / (1.0 + jnp.exp(-gate)) * up * scale[e : e + 1, r : r + LANES]
            hidden[pl.ds(e * per // 2, per // 2), r : r + LANES] = act.astype(jnp.bfloat16)
    chunk = min(512, width)
    for c in range(0, width, chunk):
        part = lax.dot_general(
            hidden[...],
            wout_ref[:, c : c + chunk],
            (((0,), (0,)), ((), ())),
            preferred_element_type=jnp.float32,
        )
        for b in range(half):
            keep_ref[b, :, c : c + chunk] = part[b * block : (b + 1) * block]
            other = part[(half + b) * block : (half + b + 1) * block]
            send_ref[b, :, c : c + chunk] = other.astype(jnp.bfloat16)


def run_experts(select, blocks, win, wout, exp_dev):
    half = len(blocks) // 2
    block_rows, packed_width = blocks[0].shape
    width = wout.shape[1]
    lines = win.shape[1]
    block = min(block_rows, max(16, 128 // half))
    rows = 2 * half * block
    out_block = pl.BlockSpec((half, block, width), lambda i: (0, i, 0))
    planned = 2 * rows * (2 * packed_width + 3 * width) + rows * (4 * lines + 4 * width)
    return pl.pallas_call(
        functools.partial(expert_kernel, exp_dev, half),
        grid=(block_rows // block,),
        out_shape=(
            jax.ShapeDtypeStruct((half, block_rows, width), jnp.bfloat16),
            jax.ShapeDtypeStruct((half, block_rows, width), jnp.float32),
        ),
        in_specs=[
            pl.BlockSpec(select.shape, lambda i: (0, 0)),
            *[pl.BlockSpec((block, packed_width), lambda i: (i, 0))] * (2 * half),
            VMEM,
            VMEM,
        ],
        out_specs=[out_block, out_block],
        scratch_shapes=[
            pltpu.VMEM((lines // exp_dev, LANES), jnp.float32),
            pltpu.VMEM((lines // 2, rows), jnp.bfloat16),
        ],
        compiler_params=pltpu.CompilerParams(vmem_limit_bytes=planned + 2 * MIB),
        cost_estimate=pl.CostEstimate(
            flops=6 * half * block_rows * width * lines,
            bytes_accessed=4 * half * block_rows * packed_width + 6 * half * block_rows * width,
            transcendentals=half * block_rows * lines,
        ),
    )(select, *blocks, win, wout)


def body(tokens, expert_ids, route_weights, in_weights, out_weights):
    tok_dev, width = tokens.shape
    exp_dev, units = in_weights.shape[:2]
    groups = lax.axis_size("expert")
    planes = lax.axis_size("batch")
    chips = groups // 2
    experts = exp_dev * groups
    far = planes - 1
    w_in = in_weights.reshape(exp_dev * units, 2, width)
    w_out = out_weights.reshape(exp_dev * units, width)

    x = pack(tokens, expert_ids, route_weights, experts)
    along = [swap(x, "expert", 2 * r) for r in range(1, chips)]
    across = swap(x, "batch", far)
    mine = stack([x] + along)
    mine, across, w_in = lax.optimization_barrier((mine, across, w_in))
    blocks = [swap(mine, "batch", b) for b in range(1, far)]
    others = [swap(across, "expert", 2 * r) for r in range(1, chips)]
    win, wout = load_weights(w_in, w_out)
    blocks, others, win = lax.optimization_barrier((blocks, others, win))
    blocks = [mine] + blocks + [stack([across] + others)]
    blocks = blocks + [swap(block, "expert", 1) for block in blocks]

    tail = x.shape[1] - width
    wanted = lax.axis_index("expert") * exp_dev + jnp.arange(exp_dev, dtype=jnp.int32)
    column = jnp.arange(tail, dtype=jnp.int32)
    select = (column[None, :] % experts == wanted[:, None]) & (column < 3 * experts)[None, :]
    select = jnp.pad(select.astype(jnp.bfloat16), ((0, -exp_dev % 16), (0, 0)))

    send, total = run_experts(select, blocks, win, wout, exp_dev)
    total = total + swap(send, "expert", 1).astype(jnp.float32)
    rounded = total.astype(jnp.bfloat16)
    mine = total[0]
    for b in range(1, far):
        mine = mine + swap(rounded[b], "batch", b).astype(jnp.float32)
    across = total[far, :tok_dev]
    for r in range(1, chips):
        piece = rounded[far, r * tok_dev : (r + 1) * tok_dev]
        across = across + swap(piece, "expert", 2 * r).astype(jnp.float32)
    result = mine[:tok_dev] + swap(across.astype(jnp.bfloat16), "batch", far).astype(jnp.float32)
    rounded = mine.astype(jnp.bfloat16)
    for r in range(1, chips):
        piece = rounded[r * tok_dev : (r + 1) * tok_dev]
        result = result + swap(piece, "expert", 2 * r).astype(jnp.float32)
    return result.astype(jnp.bfloat16)


def solution(mesh):
    return jax.shard_map(
        body,
        mesh=mesh,
        in_specs=(
            P(("batch", "expert"), None),
            P(("batch", "expert"), None),
            P(("batch", "expert"), None),
            P("expert", "batch", None, None),
            P("expert", "batch", None),
        ),
        out_specs=P(("batch", "expert"), None),
        check_vma=False,
    )
```

```python
import functools

import jax
import jax.numpy as jnp
from jax import lax
from jax.experimental import pallas as pl
from jax.experimental.pallas import tpu as pltpu
from jax.sharding import PartitionSpec as P

LANES = 128
MIB = 1 << 20
VMEM = pl.BlockSpec(memory_space=pltpu.VMEM)
HBM = pl.BlockSpec(memory_space=pltpu.HBM)


def in_hbm(*arrays):
    return [pltpu.with_memory_space_constraint(array, pltpu.HBM) for array in arrays]


def swap(block, axis, flips):
    size = lax.axis_size(axis)
    return lax.ppermute(block, axis, [(i, i ^ flips) for i in range(size)])


def pack_kernel(
    experts, tokens_hbm, ids_hbm, weights_hbm, packed_ref, tokens_ref, ids_ref, weights_ref, sems
):
    copies = [
        pltpu.make_async_copy(source, target, sems.at[i])
        for i, (source, target) in enumerate(
            ((ids_hbm, ids_ref), (weights_hbm, weights_ref), (tokens_hbm, tokens_ref))
        )
    ]
    for copy in copies:
        copy.start()
    for copy in copies:
        copy.wait()
    rows, width = tokens_ref.shape
    tail = packed_ref.shape[1] - width
    packed_ref[:, :width] = tokens_ref[...]
    lane = lax.broadcasted_iota(jnp.int32, (rows, tail), 1)
    expert = lane % experts
    part = lane // experts
    dense = jnp.zeros((rows, tail), jnp.float32)
    for k in range(ids_ref.shape[1]):
        dense += jnp.where(ids_ref[:, k : k + 1] == expert, weights_ref[:, k : k + 1], 0.0)
    result = jnp.zeros((rows, tail), jnp.float32)
    for step in range(3):
        rounded = dense.astype(jnp.bfloat16).astype(jnp.float32)
        result = jnp.where(part == step, rounded, result)
        dense = dense - rounded
    packed_ref[:, width:] = result.astype(jnp.bfloat16)


def pack(tokens, expert_ids, route_weights, experts):
    rows, width = tokens.shape
    tail = -(-3 * experts // LANES) * LANES
    return pl.pallas_call(
        functools.partial(pack_kernel, experts),
        out_shape=jax.ShapeDtypeStruct((rows, width + tail), jnp.bfloat16),
        in_specs=[HBM] * 3,
        out_specs=VMEM,
        scratch_shapes=[
            pltpu.VMEM(tokens.shape, tokens.dtype),
            pltpu.VMEM(expert_ids.shape, expert_ids.dtype),
            pltpu.VMEM(route_weights.shape, route_weights.dtype),
            pltpu.SemaphoreType.DMA((3,)),
        ],
        compiler_params=pltpu.CompilerParams(vmem_limit_bytes=2 * MIB),
    )(*in_hbm(tokens, expert_ids, route_weights))


def stack_kernel(*refs):
    out_ref = refs[-1]
    start = 0
    for ref in refs[1:-2]:
        out_ref[start : start + ref.shape[0], :] = ref[...]
        start += ref.shape[0]


def stack(win, blocks):
    rows = sum(block.shape[0] for block in blocks)
    return pl.pallas_call(
        stack_kernel,
        out_shape=(
            pltpu.VMEM(win.shape, win.dtype),
            jax.ShapeDtypeStruct((rows, blocks[0].shape[1]), blocks[0].dtype),
        ),
        in_specs=[VMEM] * (1 + len(blocks)),
        out_specs=[VMEM] * 2,
        input_output_aliases={0: 0},
        compiler_params=pltpu.CompilerParams(vmem_limit_bytes=2 * MIB),
    )(pltpu.with_memory_space_constraint(win, pltpu.VMEM), *blocks)


def load_kernel(in_ref, in_vmem, sems):
    tiles = in_vmem.shape[0]
    copies = [
        pltpu.make_async_copy(in_ref.at[:, :, pl.ds(t * LANES, LANES)], in_vmem.at[t], sems.at[t])
        for t in range(tiles)
    ]
    for copy in copies:
        copy.start()
    for copy in copies:
        copy.wait()


def load_weights(w_in):
    units, _, width = w_in.shape
    tiles = width // LANES
    loaded = pl.pallas_call(
        load_kernel,
        out_shape=pltpu.VMEM((tiles, units, 2, LANES), w_in.dtype),
        in_specs=[HBM],
        out_specs=VMEM,
        scratch_shapes=[pltpu.SemaphoreType.DMA((tiles,))],
        compiler_params=pltpu.CompilerParams(vmem_limit_bytes=2 * MIB),
        cost_estimate=pl.CostEstimate(flops=0, bytes_accessed=4 * w_in.size, transcendentals=0),
    )(*in_hbm(w_in))
    return loaded.reshape(tiles, units * 2, LANES)


def expert_kernel(exp_dev, experts, half, *refs):
    group_ref = refs[0]
    x_refs = refs[1 : 1 + 2 * half]
    win_ref, wout_hbm, send_ref, keep_ref, mixed, hidden, wout_ref, sem = refs[1 + 2 * half :]
    first = pl.program_id(0) == 0
    load = pltpu.make_async_copy(wout_hbm, wout_ref, sem)

    @pl.when(first)
    def _():
        load.start()

    lines = win_ref.shape[1]
    width = win_ref.shape[0] * LANES
    per = lines // exp_dev
    block = x_refs[0].shape[0]
    rows = 2 * half * block
    x = jnp.concatenate([ref[:, :width] for ref in x_refs], axis=0)
    tail = jnp.concatenate([ref[:, width:] for ref in x_refs], axis=0)
    contract_last = (((1,), (1,)), ((), ()))
    column = lax.broadcasted_iota(jnp.int32, (16, tail.shape[1]), 1)
    wanted = lax.broadcasted_iota(jnp.int32, (16, tail.shape[1]), 0) + group_ref[0] * exp_dev
    select = (column % experts == wanted) & (column < 3 * experts)
    scale = lax.dot_general(
        select.astype(jnp.bfloat16), tail, contract_last, preferred_element_type=jnp.float32
    )
    for e in range(exp_dev):
        w = jnp.concatenate(
            [win_ref[t, pl.ds(e * per, per), :] for t in range(win_ref.shape[0])], axis=1
        )
        both = lax.dot_general(w, x, contract_last, preferred_element_type=jnp.float32)
        for r in range(0, rows, LANES):
            mixed[...] = both[:, r : r + LANES]
            gate = mixed[pl.ds(0, per // 2, stride=2), :]
            up = mixed[pl.ds(1, per // 2, stride=2), :]
            act = gate / (1.0 + jnp.exp(-gate)) * up * scale[e : e + 1, r : r + LANES]
            hidden[pl.ds(e * per // 2, per // 2), r : r + LANES] = act.astype(jnp.bfloat16)

    @pl.when(first)
    def _():
        load.wait()

    chunk = min(512, width)
    for c in range(0, width, chunk):
        part = lax.dot_general(
            hidden[...],
            wout_ref[:, c : c + chunk],
            (((0,), (0,)), ((), ())),
            preferred_element_type=jnp.float32,
        )
        for b in range(half):
            keep_ref[b, :, c : c + chunk] = part[b * block : (b + 1) * block]
            other = part[(half + b) * block : (half + b + 1) * block]
            send_ref[b, :, c : c + chunk] = other.astype(jnp.bfloat16)


def run_experts(group, blocks, win, wout, exp_dev, experts):
    half = len(blocks) // 2
    block_rows, packed_width = blocks[0].shape
    width = wout.shape[1]
    lines = win.shape[1]
    block = min(block_rows, max(16, 128 // half))
    rows = 2 * half * block
    out_block = pl.BlockSpec((half, block, width), lambda i: (0, i, 0))
    planned = 2 * rows * (2 * packed_width + 3 * width) + rows * (4 * lines + 4 * width)
    return pl.pallas_call(
        functools.partial(expert_kernel, exp_dev, experts, half),
        grid=(block_rows // block,),
        out_shape=(
            jax.ShapeDtypeStruct((half, block_rows, width), jnp.bfloat16),
            jax.ShapeDtypeStruct((half, block_rows, width), jnp.float32),
        ),
        in_specs=[
            pl.BlockSpec(memory_space=pltpu.SMEM),
            *[pl.BlockSpec((block, packed_width), lambda i: (i, 0))] * (2 * half),
            VMEM,
            HBM,
        ],
        out_specs=[out_block, out_block],
        scratch_shapes=[
            pltpu.VMEM((lines // exp_dev, LANES), jnp.float32),
            pltpu.VMEM((lines // 2, rows), jnp.bfloat16),
            pltpu.VMEM(wout.shape, wout.dtype),
            pltpu.SemaphoreType.DMA,
        ],
        compiler_params=pltpu.CompilerParams(vmem_limit_bytes=planned + 2 * wout.size + 2 * MIB),
        cost_estimate=pl.CostEstimate(
            flops=6 * half * block_rows * width * lines,
            bytes_accessed=4 * half * block_rows * packed_width + 6 * half * block_rows * width,
            transcendentals=half * block_rows * lines,
        ),
    )(group, *blocks, pltpu.with_memory_space_constraint(win, pltpu.VMEM), *in_hbm(wout))


def body(tokens, expert_ids, route_weights, in_weights, out_weights):
    tok_dev, width = tokens.shape
    exp_dev, units = in_weights.shape[:2]
    groups = lax.axis_size("expert")
    planes = lax.axis_size("batch")
    chips = groups // 2
    experts = exp_dev * groups
    far = planes - 1
    w_in = in_weights.reshape(exp_dev * units, 2, width)
    w_out = out_weights.reshape(exp_dev * units, width)

    x = pack(tokens, expert_ids, route_weights, experts)
    group = lax.axis_index("expert").astype(jnp.int32).reshape(1)
    x, w_in, group = lax.optimization_barrier((x, w_in, group))
    along = [swap(x, "expert", 2 * r) for r in range(1, chips)]
    across = swap(x, "batch", far)
    win = load_weights(w_in)
    along, across, win = lax.optimization_barrier((along, across, win))
    win, mine = stack(win, [x] + along)
    blocks = [mine] + [swap(mine, "batch", b) for b in range(1, far)]
    others = [swap(across, "expert", 2 * r) for r in range(1, chips)]
    win, last = stack(win, [across] + others)
    blocks.append(last)
    blocks = blocks + [swap(block, "expert", 1) for block in blocks]

    send, total = run_experts(group, blocks, win, w_out, exp_dev, experts)
    total = total + swap(send, "expert", 1).astype(jnp.float32)
    rounded = total.astype(jnp.bfloat16)
    mine = total[0]
    for b in range(1, far):
        mine = mine + swap(rounded[b], "batch", b).astype(jnp.float32)
    across = total[far, :tok_dev]
    for r in range(1, chips):
        piece = rounded[far, r * tok_dev : (r + 1) * tok_dev]
        across = across + swap(piece, "expert", 2 * r).astype(jnp.float32)
    result = mine[:tok_dev] + swap(across.astype(jnp.bfloat16), "batch", far).astype(jnp.float32)
    rounded = mine.astype(jnp.bfloat16)
    for r in range(1, chips):
        piece = rounded[r * tok_dev : (r + 1) * tok_dev]
        result = result + swap(piece, "expert", 2 * r).astype(jnp.float32)
    return result.astype(jnp.bfloat16)


def solution(mesh):
    return jax.shard_map(
        body,
        mesh=mesh,
        in_specs=(
            P(("batch", "expert"), None),
            P(("batch", "expert"), None),
            P(("batch", "expert"), None),
            P("expert", "batch", None, None),
            P("expert", "batch", None),
        ),
        out_specs=P(("batch", "expert"), None),
        check_vma=False,
    )
```

```python
import functools

import jax
import jax.numpy as jnp
from jax import lax
from jax.experimental import pallas as pl
from jax.experimental.pallas import tpu as pltpu
from jax.sharding import PartitionSpec as P

LANES = 128
MIB = 1 << 20
VMEM = pl.BlockSpec(memory_space=pltpu.VMEM)
HBM = pl.BlockSpec(memory_space=pltpu.HBM)


def in_hbm(*arrays):
    return [pltpu.with_memory_space_constraint(array, pltpu.HBM) for array in arrays]


def swap(block, axis, flips):
    size = lax.axis_size(axis)
    return lax.ppermute(block, axis, [(i, i ^ flips) for i in range(size)])


def exchange(blocks):
    return lax.all_to_all(blocks, "chip", split_axis=0, concat_axis=0, tiled=True)


def pack_kernel(
    experts,
    tokens_hbm,
    ids_hbm,
    weights_hbm,
    packed_ref,
    repeated_ref,
    tokens_ref,
    ids_ref,
    weights_ref,
    sems,
):
    copies = [
        pltpu.make_async_copy(source, target, sems.at[i])
        for i, (source, target) in enumerate(
            ((ids_hbm, ids_ref), (weights_hbm, weights_ref), (tokens_hbm, tokens_ref))
        )
    ]
    for copy in copies:
        copy.start()
    for copy in copies:
        copy.wait()
    rows, width = tokens_ref.shape
    tail = packed_ref.shape[1] - width
    packed_ref[:, :width] = tokens_ref[...]
    lane = lax.broadcasted_iota(jnp.int32, (rows, tail), 1)
    expert = lane % experts
    part = lane // experts
    dense = jnp.zeros((rows, tail), jnp.float32)
    for k in range(ids_ref.shape[1]):
        dense += jnp.where(ids_ref[:, k : k + 1] == expert, weights_ref[:, k : k + 1], 0.0)
    result = jnp.zeros((rows, tail), jnp.float32)
    for step in range(3):
        rounded = dense.astype(jnp.bfloat16).astype(jnp.float32)
        result = jnp.where(part == step, rounded, result)
        dense = dense - rounded
    packed_ref[:, width:] = result.astype(jnp.bfloat16)
    for start in range(0, repeated_ref.shape[0], rows):
        repeated_ref[start : start + rows, :] = packed_ref[...]


def pack(tokens, expert_ids, route_weights, experts, times):
    rows, width = tokens.shape
    tail = -(-3 * experts // LANES) * LANES
    return pl.pallas_call(
        functools.partial(pack_kernel, experts),
        out_shape=(
            jax.ShapeDtypeStruct((rows, width + tail), jnp.bfloat16),
            jax.ShapeDtypeStruct((times * rows, width + tail), jnp.bfloat16),
        ),
        in_specs=[HBM] * 3,
        out_specs=[VMEM] * 2,
        scratch_shapes=[
            pltpu.VMEM(tokens.shape, tokens.dtype),
            pltpu.VMEM(expert_ids.shape, expert_ids.dtype),
            pltpu.VMEM(route_weights.shape, route_weights.dtype),
            pltpu.SemaphoreType.DMA((3,)),
        ],
        compiler_params=pltpu.CompilerParams(vmem_limit_bytes=2 * MIB),
    )(*in_hbm(tokens, expert_ids, route_weights))


def repeat_kernel(block_ref, out_ref):
    rows = block_ref.shape[0]
    for start in range(0, out_ref.shape[0], rows):
        out_ref[start : start + rows, :] = block_ref[...]


def repeat(block, times):
    rows, width = block.shape
    return pl.pallas_call(
        repeat_kernel,
        out_shape=jax.ShapeDtypeStruct((times * rows, width), block.dtype),
        in_specs=[VMEM],
        out_specs=VMEM,
        compiler_params=pltpu.CompilerParams(vmem_limit_bytes=2 * MIB),
    )(block)


def expert_kernel(exp_dev, experts, half, one_step, *refs):
    group_ref = refs[0]
    x_refs = refs[1 : 1 + 2 * half]
    win_hbm, wout_hbm, send_ref, keep_ref = refs[1 + 2 * half : 5 + 2 * half]
    win_pairs, wout_ref, mixed, hidden, in_sems, out_sems = refs[5 + 2 * half :]
    _, tiles, units, _, _ = win_pairs.shape
    parts, _, chunk = wout_ref.shape
    win_ref = win_pairs.reshape(exp_dev, tiles, 2 * units, LANES)
    in_loads = [
        [
            pltpu.make_async_copy(
                win_hbm.at[pl.ds(e * units, units), :, pl.ds(t * LANES, LANES)],
                win_pairs.at[e, t],
                in_sems.at[e, t],
            )
            for t in range(tiles)
        ]
        for e in range(exp_dev)
    ]
    out_loads = [
        pltpu.make_async_copy(
            wout_hbm.at[:, pl.ds(p * chunk, chunk)], wout_ref.at[p], out_sems.at[p]
        )
        for p in range(parts)
    ]

    def on_first(loads, act):
        def run():
            for load in loads:
                act(load)

        if one_step:
            run()
        else:
            pl.when(pl.program_id(0) == 0)(run)

    every = [load for loads in in_loads for load in loads] + out_loads
    on_first(every, lambda load: load.start())

    width = tiles * LANES
    block = x_refs[0].shape[0]
    rows = 2 * half * block
    tail = jnp.concatenate([ref[:, width:] for ref in x_refs], axis=0)
    contract_last = (((1,), (1,)), ((), ()))
    column = lax.broadcasted_iota(jnp.int32, (16, tail.shape[1]), 1)
    wanted = lax.broadcasted_iota(jnp.int32, (16, tail.shape[1]), 0) + group_ref[0] * exp_dev
    select = (column % experts == wanted) & (column < 3 * experts)
    scale = lax.dot_general(
        select.astype(jnp.bfloat16), tail, contract_last, preferred_element_type=jnp.float32
    )
    step = tiles // 2
    for e in range(exp_dev):
        both = 0.0
        for t in range(0, tiles, step):
            on_first(in_loads[e][t : t + step], lambda load: load.wait())
            w = jnp.concatenate([win_ref[e, u] for u in range(t, t + step)], axis=1)
            lanes = slice(t * LANES, (t + step) * LANES)
            x = jnp.concatenate([ref[:, lanes] for ref in x_refs], axis=0)
            both += lax.dot_general(w, x, contract_last, preferred_element_type=jnp.float32)
        for r in range(0, rows, LANES):
            mixed[...] = both[:, r : r + LANES]
            gate = mixed[pl.ds(0, units, stride=2), :]
            up = mixed[pl.ds(1, units, stride=2), :]
            act = gate / (1.0 + jnp.exp(-gate)) * up * scale[e : e + 1, r : r + LANES]
            hidden[pl.ds(e * units, units), r : r + LANES] = act.astype(jnp.bfloat16)
    for p in range(parts):
        on_first(out_loads[p : p + 1], lambda load: load.wait())
        part = lax.dot_general(
            hidden[...],
            wout_ref[p],
            (((0,), (0,)), ((), ())),
            preferred_element_type=jnp.float32,
        )
        lanes = slice(p * chunk, (p + 1) * chunk)
        for b in range(half):
            keep_ref[b, :, lanes] = part[b * block : (b + 1) * block]
            other = part[(half + b) * block : (half + b + 1) * block]
            send_ref[b, :, lanes] = other.astype(jnp.bfloat16)


def run_experts(group, blocks, win, wout, exp_dev, experts):
    half = len(blocks) // 2
    block_rows, packed_width = blocks[0].shape
    lines, width = wout.shape
    tiles = width // LANES
    parts = 4
    block = min(block_rows, max(16, 128 // half))
    rows = 2 * half * block
    steps = block_rows // block
    if steps == 1:
        x_block, out_block, grid = VMEM, VMEM, ()
    else:
        x_block = pl.BlockSpec((block, packed_width), lambda i: (i, 0))
        out_block = pl.BlockSpec((half, block, width), lambda i: (0, i, 0))
        grid = (steps,)
    windows = 0 if steps == 1 else 2 * rows * (2 * packed_width + 3 * width)
    scratch = 2 * (win.size + wout.size) + rows * (10 * lines + 6 * width)
    return pl.pallas_call(
        functools.partial(expert_kernel, exp_dev, experts, half, steps == 1),
        grid=grid,
        out_shape=(
            jax.ShapeDtypeStruct((half, block_rows, width), jnp.bfloat16),
            jax.ShapeDtypeStruct((half, block_rows, width), jnp.float32),
        ),
        in_specs=[
            pl.BlockSpec(memory_space=pltpu.SMEM),
            *[x_block] * (2 * half),
            HBM,
            HBM,
        ],
        out_specs=[out_block, out_block],
        scratch_shapes=[
            pltpu.VMEM((exp_dev, tiles, lines // exp_dev, 2, LANES), win.dtype),
            pltpu.VMEM((parts, lines, width // parts), wout.dtype),
            pltpu.VMEM((2 * lines // exp_dev, LANES), jnp.float32),
            pltpu.VMEM((lines, rows), jnp.bfloat16),
            pltpu.SemaphoreType.DMA((exp_dev, tiles)),
            pltpu.SemaphoreType.DMA((parts,)),
        ],
        compiler_params=pltpu.CompilerParams(vmem_limit_bytes=windows + scratch + 4 * MIB),
        cost_estimate=pl.CostEstimate(
            flops=12 * half * block_rows * width * lines,
            bytes_accessed=4 * half * block_rows * packed_width + 6 * half * block_rows * width,
            transcendentals=2 * half * block_rows * lines,
        ),
    )(group, *blocks, *in_hbm(win, wout))


def body(tokens, expert_ids, route_weights, in_weights, out_weights):
    tok_dev, width = tokens.shape
    exp_dev, units = in_weights.shape[:2]
    planes = lax.axis_size("batch")
    chips = lax.axis_size("chip")
    experts = exp_dev * lax.axis_size("core") * chips
    far = planes - 1
    w_in = in_weights.reshape(exp_dev * units, 2, width)
    w_out = out_weights.reshape(exp_dev * units, width)

    group = lax.axis_index(("chip", "core")).astype(jnp.int32).reshape(1)
    x, repeated = pack(tokens, expert_ids, route_weights, experts, chips)
    across = swap(x, "batch", far)
    mine = exchange(repeated)
    blocks = [mine] + [swap(mine, "batch", b) for b in range(1, far)]
    blocks.append(exchange(repeat(across, chips)))
    blocks = blocks + [swap(block, "core", 1) for block in blocks]

    send, total = run_experts(group, blocks, w_in, w_out, exp_dev, experts)
    total = total + swap(send, "core", 1).astype(jnp.float32)
    rounded = total.astype(jnp.bfloat16)
    mine = total[0]
    for b in range(1, far):
        mine = mine + swap(rounded[b], "batch", b).astype(jnp.float32)
    across = exchange(rounded[far]).reshape(chips, tok_dev, width).astype(jnp.float32).sum(0)
    across = swap(across.astype(jnp.bfloat16), "batch", far)
    mine = exchange(mine.astype(jnp.bfloat16)).reshape(chips, tok_dev, width)
    result = mine.astype(jnp.float32).sum(0) + across.astype(jnp.float32)
    return result.astype(jnp.bfloat16)


def solution(mesh):
    planes, groups = mesh.devices.shape
    mesh = jax.sharding.Mesh(
        mesh.devices.reshape(planes, groups // 2, 2), ("batch", "chip", "core")
    )
    expert = ("chip", "core")
    tokens = P(("batch",) + expert, None)
    return jax.shard_map(
        body,
        mesh=mesh,
        in_specs=(
            tokens,
            tokens,
            tokens,
            P(expert, "batch", None, None),
            P(expert, "batch", None),
        ),
        out_specs=tokens,
        check_vma=False,
    )
```

```python
import functools

import jax
import jax.numpy as jnp
from jax import lax
from jax.experimental import pallas as pl
from jax.experimental.pallas import tpu as pltpu
from jax.sharding import PartitionSpec as P

LANES = 128
MIB = 1 << 20
VMEM = pl.BlockSpec(memory_space=pltpu.VMEM)
HBM = pl.BlockSpec(memory_space=pltpu.HBM)


def in_hbm(*arrays):
    return [pltpu.with_memory_space_constraint(array, pltpu.HBM) for array in arrays]


def swap(block, axis, flips):
    size = lax.axis_size(axis)
    return lax.ppermute(block, axis, [(i, i ^ flips) for i in range(size)])


def pack_kernel(
    experts, tokens_hbm, ids_hbm, weights_hbm, packed_ref, tokens_ref, ids_ref, weights_ref, sems
):
    copies = [
        pltpu.make_async_copy(source, target, sems.at[i])
        for i, (source, target) in enumerate(
            ((ids_hbm, ids_ref), (weights_hbm, weights_ref), (tokens_hbm, tokens_ref))
        )
    ]
    for copy in copies:
        copy.start()
    for copy in copies:
        copy.wait()
    rows, width = tokens_ref.shape
    tail = packed_ref.shape[1] - width
    packed_ref[:, :width] = tokens_ref[...]
    lane = lax.broadcasted_iota(jnp.int32, (rows, tail), 1)
    expert = lane % experts
    part = lane // experts
    dense = jnp.zeros((rows, tail), jnp.float32)
    for k in range(ids_ref.shape[1]):
        dense += jnp.where(ids_ref[:, k : k + 1] == expert, weights_ref[:, k : k + 1], 0.0)
    result = jnp.zeros((rows, tail), jnp.float32)
    for step in range(3):
        rounded = dense.astype(jnp.bfloat16).astype(jnp.float32)
        result = jnp.where(part == step, rounded, result)
        dense = dense - rounded
    packed_ref[:, width:] = result.astype(jnp.bfloat16)


def pack(tokens, expert_ids, route_weights, experts):
    rows, width = tokens.shape
    tail = -(-3 * experts // LANES) * LANES
    return pl.pallas_call(
        functools.partial(pack_kernel, experts),
        out_shape=jax.ShapeDtypeStruct((rows, width + tail), jnp.bfloat16),
        in_specs=[HBM] * 3,
        out_specs=VMEM,
        scratch_shapes=[
            pltpu.VMEM(tokens.shape, tokens.dtype),
            pltpu.VMEM(expert_ids.shape, expert_ids.dtype),
            pltpu.VMEM(route_weights.shape, route_weights.dtype),
            pltpu.SemaphoreType.DMA((3,)),
        ],
        compiler_params=pltpu.CompilerParams(vmem_limit_bytes=2 * MIB),
    )(*in_hbm(tokens, expert_ids, route_weights))


def stack_kernel(first_ref, second_ref, out_ref):
    rows = first_ref.shape[0]
    out_ref[:rows, :] = first_ref[...]
    out_ref[rows:, :] = second_ref[...]


def stack(first, second):
    rows, width = first.shape
    return pl.pallas_call(
        stack_kernel,
        out_shape=jax.ShapeDtypeStruct((rows + second.shape[0], width), first.dtype),
        in_specs=[VMEM] * 2,
        out_specs=VMEM,
        compiler_params=pltpu.CompilerParams(vmem_limit_bytes=2 * MIB),
    )(first, second)


def load_kernel(in_ref, in_vmem, sems):
    tiles = in_vmem.shape[0]
    copies = [
        pltpu.make_async_copy(in_ref.at[:, :, pl.ds(t * LANES, LANES)], in_vmem.at[t], sems.at[t])
        for t in range(tiles)
    ]
    for copy in copies:
        copy.start()
    for copy in copies:
        copy.wait()


def load_weights(w_in):
    units, _, width = w_in.shape
    tiles = width // LANES
    loaded = pl.pallas_call(
        load_kernel,
        out_shape=pltpu.VMEM((tiles, units, 2, LANES), w_in.dtype),
        in_specs=[HBM],
        out_specs=VMEM,
        scratch_shapes=[pltpu.SemaphoreType.DMA((tiles,))],
        compiler_params=pltpu.CompilerParams(vmem_limit_bytes=2 * MIB),
        cost_estimate=pl.CostEstimate(flops=0, bytes_accessed=4 * w_in.size, transcendentals=0),
    )(*in_hbm(w_in))
    return loaded.reshape(tiles, units * 2, LANES)


def expert_kernel(exp_dev, experts, count, one_step, *refs):
    group_ref = refs[0]
    x_refs = refs[1 : 1 + count]
    win_ref, wout_hbm, send_ref, keep_ref, mixed, hidden, wout_ref, sem = refs[1 + count :]
    load = pltpu.make_async_copy(wout_hbm, wout_ref, sem)
    if one_step:
        load.start()
    else:
        pl.when(pl.program_id(0) == 0)(load.start)
    tiles, lines, _ = win_ref.shape
    width = tiles * LANES
    per = lines // exp_dev
    rows = sum(ref.shape[0] for ref in x_refs)
    x = jnp.concatenate([ref[:, :width] for ref in x_refs], axis=0)
    tail = jnp.concatenate([ref[:, width:] for ref in x_refs], axis=0)
    contract_last = (((1,), (1,)), ((), ()))
    column = lax.broadcasted_iota(jnp.int32, (16, tail.shape[1]), 1)
    wanted = lax.broadcasted_iota(jnp.int32, (16, tail.shape[1]), 0) + group_ref[0] * exp_dev
    select = (column % experts == wanted) & (column < 3 * experts)
    scale = lax.dot_general(
        select.astype(jnp.bfloat16), tail, contract_last, preferred_element_type=jnp.float32
    )
    for e in range(exp_dev):
        w = jnp.concatenate([win_ref[t, pl.ds(e * per, per), :] for t in range(tiles)], axis=1)
        both = lax.dot_general(w, x, contract_last, preferred_element_type=jnp.float32)
        for r in range(0, rows, LANES):
            mixed[...] = both[:, r : r + LANES]
            gate = mixed[pl.ds(0, per // 2, stride=2), :]
            up = mixed[pl.ds(1, per // 2, stride=2), :]
            act = gate / (1.0 + jnp.exp(-gate)) * up * scale[e : e + 1, r : r + LANES]
            hidden[pl.ds(e * per // 2, per // 2), r : r + LANES] = act.astype(jnp.bfloat16)
    if one_step:
        load.wait()
    else:
        pl.when(pl.program_id(0) == 0)(load.wait)
    chunk = min(512, width)
    pieces, piece, _ = keep_ref.shape
    for c in range(0, width, chunk):
        part = lax.dot_general(
            hidden[...],
            wout_ref[:, c : c + chunk],
            (((0,), (0,)), ((), ())),
            preferred_element_type=jnp.float32,
        )
        for p in range(pieces):
            keep_ref[p, :, c : c + chunk] = part[p * piece : (p + 1) * piece]
            other = part[(pieces + p) * piece : (pieces + p + 1) * piece]
            send_ref[p, :, c : c + chunk] = other.astype(jnp.bfloat16)


def run_experts(group, blocks, win, wout, exp_dev, experts):
    packed_width = blocks[0].shape[1]
    half_rows = sum(block.shape[0] for block in blocks) // 2
    count = len(blocks)
    width = wout.shape[1]
    lines = win.shape[1]
    one_step = half_rows <= LANES
    if one_step:
        x_block, out_block, grid = VMEM, VMEM, ()
        pieces, piece, rows = 1, half_rows, 2 * half_rows
        windows = 0
    else:
        pieces, piece, block = count // 2, blocks[0].shape[0], 16
        x_block = pl.BlockSpec((block, packed_width), lambda i: (i, 0))
        out_block = pl.BlockSpec((pieces, block, width), lambda i: (0, i, 0))
        grid = (piece // block,)
        rows = count * block
        windows = 2 * rows * (2 * packed_width + 3 * width)
    scratch = 2 * wout.size + rows * (6 * lines + 6 * width)
    send, keep = pl.pallas_call(
        functools.partial(expert_kernel, exp_dev, experts, count, one_step),
        grid=grid,
        out_shape=(
            jax.ShapeDtypeStruct((pieces, piece, width), jnp.bfloat16),
            jax.ShapeDtypeStruct((pieces, piece, width), jnp.float32),
        ),
        in_specs=[pl.BlockSpec(memory_space=pltpu.SMEM), *[x_block] * count, VMEM, HBM],
        out_specs=[out_block, out_block],
        scratch_shapes=[
            pltpu.VMEM((lines // exp_dev, LANES), jnp.float32),
            pltpu.VMEM((lines // 2, rows), jnp.bfloat16),
            pltpu.VMEM(wout.shape, wout.dtype),
            pltpu.SemaphoreType.DMA,
        ],
        compiler_params=pltpu.CompilerParams(vmem_limit_bytes=windows + scratch + 4 * MIB),
        cost_estimate=pl.CostEstimate(
            flops=6 * half_rows * width * lines,
            bytes_accessed=4 * half_rows * packed_width + 6 * half_rows * width,
            transcendentals=half_rows * lines,
        ),
    )(group, *blocks, pltpu.with_memory_space_constraint(win, pltpu.VMEM), *in_hbm(wout))
    return send.reshape(half_rows, width), keep.reshape(half_rows, width)


def body(tokens, expert_ids, route_weights, in_weights, out_weights):
    width = tokens.shape[1]
    exp_dev, units = in_weights.shape[:2]
    groups = lax.axis_size("expert")
    planes = lax.axis_size("batch")
    experts = exp_dev * groups
    far = planes - 1
    strides = [groups >> i for i in range(1, groups.bit_length() - 1)]
    w_in = in_weights.reshape(exp_dev * units, 2, width)
    w_out = out_weights.reshape(exp_dev * units, width)

    group = lax.axis_index("expert").astype(jnp.int32).reshape(1)
    x = pack(tokens, expert_ids, route_weights, experts)
    x, group = lax.optimization_barrier((x, group))
    for stride in strides[:-1]:
        x = stack(x, swap(x, "expert", stride))
    across = swap(x, "batch", far)
    mine = stack(x, swap(x, "expert", strides[-1]))
    mine, across, w_in = lax.optimization_barrier((mine, across, w_in))
    early = [mine, across]
    late = [swap(mine, "batch", b) for b in range(1, far)]
    late.append(swap(across, "expert", strides[-1]))
    early_core = [swap(block, "expert", 1) for block in early]
    win = load_weights(w_in)
    late, win = lax.optimization_barrier((late, win))
    late_core = [swap(block, "expert", 1) for block in late]
    blocks = []
    for (mine, across), rest in ((early, late), (early_core, late_core)):
        if 2 * mine.shape[0] * planes <= 2 * LANES:
            blocks += [mine] + rest[:-1] + [across, rest[-1]]
        else:
            blocks += [mine] + rest[:-1] + [jnp.concatenate([across, rest[-1]], axis=0)]

    send, total = run_experts(group, blocks, win, w_out, exp_dev, experts)
    total = total + swap(send, "expert", 1).astype(jnp.float32)
    size = total.shape[0] // planes
    rounded = total.astype(jnp.bfloat16)
    mine = total[:size]
    for b in range(1, far):
        piece = rounded[b * size : (b + 1) * size]
        mine = mine + swap(piece, "batch", b).astype(jnp.float32)
    size = size // 2
    piece = rounded[2 * far * size + size :]
    across = total[2 * far * size : 2 * far * size + size]
    across = across + swap(piece, "expert", strides[-1]).astype(jnp.float32)
    piece = mine[size:].astype(jnp.bfloat16)
    mine = mine[:size] + swap(piece, "expert", strides[-1]).astype(jnp.float32)
    mine = mine + swap(across.astype(jnp.bfloat16), "batch", far).astype(jnp.float32)
    for stride in reversed(strides[:-1]):
        size = size // 2
        piece = mine[size:].astype(jnp.bfloat16)
        mine = mine[:size] + swap(piece, "expert", stride).astype(jnp.float32)
    return mine.astype(jnp.bfloat16)


def solution(mesh):
    return jax.shard_map(
        body,
        mesh=mesh,
        in_specs=(
            P(("batch", "expert"), None),
            P(("batch", "expert"), None),
            P(("batch", "expert"), None),
            P("expert", "batch", None, None),
            P("expert", "batch", None),
        ),
        out_specs=P(("batch", "expert"), None),
        check_vma=False,
    )
```

```python
import functools
import math

import jax
import jax.numpy as jnp
from jax import lax
from jax.experimental import pallas as pl
from jax.experimental.pallas import tpu as pltpu
from jax.sharding import PartitionSpec as P

LANES = 128
MIB = 1 << 20
VMEM = pl.BlockSpec(memory_space=pltpu.VMEM)
HBM = pl.BlockSpec(memory_space=pltpu.HBM)


def in_hbm(*arrays):
    return [pltpu.with_memory_space_constraint(array, pltpu.HBM) for array in arrays]


def in_vmem(*arrays):
    return [pltpu.with_memory_space_constraint(array, pltpu.VMEM) for array in arrays]


def swap(block, axis, flips):
    size = lax.axis_size(axis)
    return lax.ppermute(block, axis, [(i, i ^ flips) for i in range(size)])


def pack_kernel(
    experts, tokens_hbm, ids_hbm, weights_hbm, packed_ref, tokens_ref, ids_ref, weights_ref, sems
):
    copies = [
        pltpu.make_async_copy(source, target, sems.at[i])
        for i, (source, target) in enumerate(
            ((ids_hbm, ids_ref), (weights_hbm, weights_ref), (tokens_hbm, tokens_ref))
        )
    ]
    for copy in copies:
        copy.start()
    for copy in copies:
        copy.wait()
    rows, width = tokens_ref.shape
    tail = packed_ref.shape[1] - width
    packed_ref[:, :width] = tokens_ref[...]
    lane = lax.broadcasted_iota(jnp.int32, (rows, tail), 1)
    expert = lane % experts
    part = lane // experts
    dense = jnp.zeros((rows, tail), jnp.float32)
    for k in range(ids_ref.shape[1]):
        dense += jnp.where(ids_ref[:, k : k + 1] == expert, weights_ref[:, k : k + 1], 0.0)
    result = jnp.zeros((rows, tail), jnp.float32)
    for step in range(3):
        rounded = dense.astype(jnp.bfloat16).astype(jnp.float32)
        result = jnp.where(part == step, rounded, result)
        dense = dense - rounded
    packed_ref[:, width:] = result.astype(jnp.bfloat16)


def pack(tokens, expert_ids, route_weights, experts):
    rows, width = tokens.shape
    tail = -(-3 * experts // LANES) * LANES
    return pl.pallas_call(
        functools.partial(pack_kernel, experts),
        out_shape=jax.ShapeDtypeStruct((rows, width + tail), jnp.bfloat16),
        in_specs=[HBM] * 3,
        out_specs=VMEM,
        scratch_shapes=[
            pltpu.VMEM(tokens.shape, tokens.dtype),
            pltpu.VMEM(expert_ids.shape, expert_ids.dtype),
            pltpu.VMEM(route_weights.shape, route_weights.dtype),
            pltpu.SemaphoreType.DMA((3,)),
        ],
        compiler_params=pltpu.CompilerParams(vmem_limit_bytes=2 * MIB),
    )(*in_hbm(tokens, expert_ids, route_weights))


def stack_kernel(count, first_ref, second_ref, *refs):
    out_ref = refs[count]
    rows = first_ref.shape[0]
    out_ref[:rows, :] = first_ref[...]
    out_ref[rows:, :] = second_ref[...]


def stack(first, second, held):
    rows, width = first.shape
    return pl.pallas_call(
        functools.partial(stack_kernel, len(held)),
        out_shape=[jax.ShapeDtypeStruct((rows + second.shape[0], width), first.dtype)]
        + [pltpu.VMEM(array.shape, array.dtype) for array in held],
        in_specs=[VMEM] * (2 + len(held)),
        out_specs=[VMEM] * (1 + len(held)),
        input_output_aliases={2 + i: 1 + i for i in range(len(held))},
        compiler_params=pltpu.CompilerParams(vmem_limit_bytes=2 * MIB),
    )(first, second, *in_vmem(*held))


def load_in_kernel(first, in_ref, in_vmem, sems):
    copies = [
        pltpu.make_async_copy(
            in_ref.at[:, :, pl.ds((first + t) * LANES, LANES)], in_vmem.at[t], sems.at[t]
        )
        for t in range(in_vmem.shape[0])
    ]
    for copy in copies:
        copy.start()
    for copy in copies:
        copy.wait()


def load_out_kernel(out_ref, out_vmem, sems):
    copies = []
    step = out_ref.shape[0] // sems.shape[0]
    for i in range(sems.shape[0]):
        rows = pl.ds(i * step, step)
        copies.append(pltpu.make_async_copy(out_ref.at[rows], out_vmem.at[rows], sems.at[i]))
    for copy in copies:
        copy.start()
    for copy in copies:
        copy.wait()


def load(kernel, source, shape, copies):
    return pl.pallas_call(
        kernel,
        out_shape=pltpu.VMEM(shape, source.dtype),
        in_specs=[HBM],
        out_specs=VMEM,
        scratch_shapes=[pltpu.SemaphoreType.DMA((copies,))],
        compiler_params=pltpu.CompilerParams(vmem_limit_bytes=2 * MIB),
        cost_estimate=pl.CostEstimate(
            flops=0, bytes_accessed=4 * math.prod(shape), transcendentals=0
        ),
    )(*in_hbm(source))


def load_in(w_in, first, tiles):
    units = w_in.shape[0]
    kernel = functools.partial(load_in_kernel, first)
    loaded = load(kernel, w_in, (tiles, units, 2, LANES), tiles)
    return loaded.reshape(tiles, 2 * units, LANES)


def expert_kernel(exp_dev, experts, count, *refs):
    group_ref = refs[0]
    x_refs = refs[1 : 1 + count]
    low_ref, high_ref, wout_ref, send_ref, keep_ref, mixed, hidden = refs[1 + count :]
    lines = low_ref.shape[1]
    width = wout_ref.shape[1]
    per = lines // exp_dev
    rows = sum(ref.shape[0] for ref in x_refs)
    x = jnp.concatenate([ref[:, :width] for ref in x_refs], axis=0)
    tail = jnp.concatenate([ref[:, width:] for ref in x_refs], axis=0)
    contract_last = (((1,), (1,)), ((), ()))
    column = lax.broadcasted_iota(jnp.int32, (16, tail.shape[1]), 1)
    wanted = lax.broadcasted_iota(jnp.int32, (16, tail.shape[1]), 0) + group_ref[0] * exp_dev
    select = (column % experts == wanted) & (column < 3 * experts)
    scale = lax.dot_general(
        select.astype(jnp.bfloat16), tail, contract_last, preferred_element_type=jnp.float32
    )
    for e in range(exp_dev):
        w = jnp.concatenate(
            [
                ref[t, pl.ds(e * per, per), :]
                for ref in (low_ref, high_ref)
                for t in range(ref.shape[0])
            ],
            axis=1,
        )
        both = lax.dot_general(w, x, contract_last, preferred_element_type=jnp.float32)
        for r in range(0, rows, LANES):
            mixed[...] = both[:, r : r + LANES]
            gate = mixed[pl.ds(0, per // 2, stride=2), :]
            up = mixed[pl.ds(1, per // 2, stride=2), :]
            act = gate / (1.0 + jnp.exp(-gate)) * up * scale[e : e + 1, r : r + LANES]
            hidden[pl.ds(e * per // 2, per // 2), r : r + LANES] = act.astype(jnp.bfloat16)
    chunk = min(512, width)
    pieces, piece, _ = keep_ref.shape
    for c in range(0, width, chunk):
        part = lax.dot_general(
            hidden[...],
            wout_ref[:, c : c + chunk],
            (((0,), (0,)), ((), ())),
            preferred_element_type=jnp.float32,
        )
        for p in range(pieces):
            keep_ref[p, :, c : c + chunk] = part[p * piece : (p + 1) * piece]
            other = part[(pieces + p) * piece : (pieces + p + 1) * piece]
            send_ref[p, :, c : c + chunk] = other.astype(jnp.bfloat16)


def run_experts(group, blocks, low, high, wout, exp_dev, experts):
    packed_width = blocks[0].shape[1]
    half_rows = sum(block.shape[0] for block in blocks) // 2
    count = len(blocks)
    width = wout.shape[1]
    lines = low.shape[1]
    one_step = half_rows <= LANES
    if one_step:
        x_block, out_block, grid = VMEM, VMEM, ()
        pieces, piece, rows = 1, half_rows, 2 * half_rows
        windows = 0
    else:
        pieces, piece, block = count // 2, blocks[0].shape[0], 16
        x_block = pl.BlockSpec((block, packed_width), lambda i: (i, 0))
        out_block = pl.BlockSpec((pieces, block, width), lambda i: (0, i, 0))
        grid = (piece // block,)
        rows = count * block
        windows = 2 * rows * (2 * packed_width + 3 * width)
    scratch = rows * (6 * lines + 6 * width)
    send, keep = pl.pallas_call(
        functools.partial(expert_kernel, exp_dev, experts, count),
        grid=grid,
        out_shape=(
            jax.ShapeDtypeStruct((pieces, piece, width), jnp.bfloat16),
            jax.ShapeDtypeStruct((pieces, piece, width), jnp.float32),
        ),
        in_specs=[pl.BlockSpec(memory_space=pltpu.SMEM), *[x_block] * count, VMEM, VMEM, VMEM],
        out_specs=[out_block, out_block],
        scratch_shapes=[
            pltpu.VMEM((lines // exp_dev, LANES), jnp.float32),
            pltpu.VMEM((lines // 2, rows), jnp.bfloat16),
        ],
        compiler_params=pltpu.CompilerParams(vmem_limit_bytes=windows + scratch + 4 * MIB),
        cost_estimate=pl.CostEstimate(
            flops=6 * half_rows * width * lines,
            bytes_accessed=4 * half_rows * packed_width + 6 * half_rows * width,
            transcendentals=half_rows * lines,
        ),
    )(group, *blocks, *in_vmem(low, high, wout))
    return send.reshape(half_rows, width), keep.reshape(half_rows, width)


def body(tokens, expert_ids, route_weights, in_weights, out_weights):
    width = tokens.shape[1]
    exp_dev, units = in_weights.shape[:2]
    groups = lax.axis_size("expert")
    planes = lax.axis_size("batch")
    experts = exp_dev * groups
    far = planes - 1
    strides = [groups >> i for i in range(1, groups.bit_length() - 1)]
    w_in = in_weights.reshape(exp_dev * units, 2, width)
    w_out = out_weights.reshape(exp_dev * units, width)

    group = lax.axis_index("expert").astype(jnp.int32).reshape(1)
    x = pack(tokens, expert_ids, route_weights, experts)
    x, group, w_in, w_out = lax.optimization_barrier((x, group, w_in, w_out))
    tiles = width // LANES
    wout = load(load_out_kernel, w_out, w_out.shape, 8)
    for stride in strides[:-1]:
        x, wout = stack(x, swap(x, "expert", stride), [wout])
    x, w_in = lax.optimization_barrier((x, w_in))
    across = swap(x, "batch", far)
    mine = swap(x, "expert", strides[-1])
    low = load_in(w_in, 0, tiles // 2)
    across, mine, low = lax.optimization_barrier((across, mine, low))
    mine, wout, low = stack(x, mine, [wout, low])
    mine, across, w_in = lax.optimization_barrier((mine, across, w_in))
    early = [mine, across]
    late = [swap(mine, "batch", b) for b in range(1, far)]
    late.append(swap(across, "expert", strides[-1]))
    early_core = [swap(block, "expert", 1) for block in early]
    high = load_in(w_in, tiles // 2, tiles - tiles // 2)
    late, high = lax.optimization_barrier((late, high))
    late_core = [swap(block, "expert", 1) for block in late]
    blocks = []
    for (mine, across), rest in ((early, late), (early_core, late_core)):
        if 2 * mine.shape[0] * planes <= 2 * LANES:
            blocks += [mine] + rest[:-1] + [across, rest[-1]]
        else:
            blocks += [mine] + rest[:-1] + [jnp.concatenate([across, rest[-1]], axis=0)]

    send, total = run_experts(group, blocks, low, high, wout, exp_dev, experts)
    total = total + swap(send, "expert", 1).astype(jnp.float32)
    size = total.shape[0] // planes
    rounded = total.astype(jnp.bfloat16)
    mine = total[:size]
    for b in range(1, far):
        piece = rounded[b * size : (b + 1) * size]
        mine = mine + swap(piece, "batch", b).astype(jnp.float32)
    size = size // 2
    piece = rounded[2 * far * size + size :]
    across = total[2 * far * size : 2 * far * size + size]
    across = across + swap(piece, "expert", strides[-1]).astype(jnp.float32)
    piece = mine[size:].astype(jnp.bfloat16)
    mine = mine[:size] + swap(piece, "expert", strides[-1]).astype(jnp.float32)
    mine = mine + swap(across.astype(jnp.bfloat16), "batch", far).astype(jnp.float32)
    for stride in reversed(strides[:-1]):
        size = size // 2
        piece = mine[size:].astype(jnp.bfloat16)
        mine = mine[:size] + swap(piece, "expert", stride).astype(jnp.float32)
    return mine.astype(jnp.bfloat16)


def solution(mesh):
    return jax.shard_map(
        body,
        mesh=mesh,
        in_specs=(
            P(("batch", "expert"), None),
            P(("batch", "expert"), None),
            P(("batch", "expert"), None),
            P("expert", "batch", None, None),
            P("expert", "batch", None),
        ),
        out_specs=P(("batch", "expert"), None),
        check_vma=False,
    )
```

```python
import functools
import math

import jax
import jax.numpy as jnp
from jax import lax
from jax.experimental import pallas as pl
from jax.experimental.pallas import tpu as pltpu
from jax.sharding import PartitionSpec as P

LANES = 128
MIB = 1 << 20
VMEM = pl.BlockSpec(memory_space=pltpu.VMEM)
HBM = pl.BlockSpec(memory_space=pltpu.HBM)


def in_hbm(*arrays):
    return [pltpu.with_memory_space_constraint(array, pltpu.HBM) for array in arrays]


def in_vmem(*arrays):
    return [pltpu.with_memory_space_constraint(array, pltpu.VMEM) for array in arrays]


def swap(block, axis, flips):
    size = lax.axis_size(axis)
    return lax.ppermute(block, axis, [(i, i ^ flips) for i in range(size)])


def pack_kernel(
    experts, tokens_hbm, ids_hbm, weights_hbm, packed_ref, tokens_ref, ids_ref, weights_ref, sems
):
    copies = [
        pltpu.make_async_copy(source, target, sems.at[i])
        for i, (source, target) in enumerate(
            ((ids_hbm, ids_ref), (weights_hbm, weights_ref), (tokens_hbm, tokens_ref))
        )
    ]
    for copy in copies:
        copy.start()
    for copy in copies:
        copy.wait()
    rows, width = tokens_ref.shape
    tail = packed_ref.shape[1] - width
    packed_ref[:, :width] = tokens_ref[...]
    lane = lax.broadcasted_iota(jnp.int32, (rows, tail), 1)
    expert = lane % experts
    part = lane // experts
    dense = jnp.zeros((rows, tail), jnp.float32)
    for k in range(ids_ref.shape[1]):
        dense += jnp.where(ids_ref[:, k : k + 1] == expert, weights_ref[:, k : k + 1], 0.0)
    result = jnp.zeros((rows, tail), jnp.float32)
    for step in range(3):
        rounded = dense.astype(jnp.bfloat16).astype(jnp.float32)
        result = jnp.where(part == step, rounded, result)
        dense = dense - rounded
    packed_ref[:, width:] = result.astype(jnp.bfloat16)


def pack(tokens, expert_ids, route_weights, experts):
    rows, width = tokens.shape
    tail = -(-3 * experts // LANES) * LANES
    return pl.pallas_call(
        functools.partial(pack_kernel, experts),
        out_shape=jax.ShapeDtypeStruct((rows, width + tail), jnp.bfloat16),
        in_specs=[HBM] * 3,
        out_specs=VMEM,
        scratch_shapes=[
            pltpu.VMEM(tokens.shape, tokens.dtype),
            pltpu.VMEM(expert_ids.shape, expert_ids.dtype),
            pltpu.VMEM(route_weights.shape, route_weights.dtype),
            pltpu.SemaphoreType.DMA((3,)),
        ],
        compiler_params=pltpu.CompilerParams(vmem_limit_bytes=2 * MIB),
    )(*in_hbm(tokens, expert_ids, route_weights))


def stack_kernel(count, first_ref, second_ref, *refs):
    out_ref = refs[count]
    rows = first_ref.shape[0]
    out_ref[:rows, :] = first_ref[...]
    out_ref[rows:, :] = second_ref[...]


def stack(first, second, held):
    rows, width = first.shape
    return pl.pallas_call(
        functools.partial(stack_kernel, len(held)),
        out_shape=[jax.ShapeDtypeStruct((rows + second.shape[0], width), first.dtype)]
        + [pltpu.VMEM(array.shape, array.dtype) for array in held],
        in_specs=[VMEM] * (2 + len(held)),
        out_specs=[VMEM] * (1 + len(held)),
        input_output_aliases={2 + i: 1 + i for i in range(len(held))},
        compiler_params=pltpu.CompilerParams(vmem_limit_bytes=2 * MIB),
    )(first, second, *in_vmem(*held))


def load_in_kernel(first, in_ref, in_vmem, sems):
    copies = [
        pltpu.make_async_copy(
            in_ref.at[:, :, pl.ds((first + t) * LANES, LANES)], in_vmem.at[t], sems.at[t]
        )
        for t in range(in_vmem.shape[0])
    ]
    for copy in copies:
        copy.start()
    for copy in copies:
        copy.wait()


def load_out_kernel(out_ref, out_vmem, sems):
    copies = []
    step = out_ref.shape[0] // sems.shape[0]
    for i in range(sems.shape[0]):
        rows = pl.ds(i * step, step)
        copies.append(pltpu.make_async_copy(out_ref.at[rows], out_vmem.at[rows], sems.at[i]))
    for copy in copies:
        copy.start()
    for copy in copies:
        copy.wait()


def load(kernel, source, shape, copies):
    return pl.pallas_call(
        kernel,
        out_shape=pltpu.VMEM(shape, source.dtype),
        in_specs=[HBM],
        out_specs=VMEM,
        scratch_shapes=[pltpu.SemaphoreType.DMA((copies,))],
        compiler_params=pltpu.CompilerParams(vmem_limit_bytes=2 * MIB),
        cost_estimate=pl.CostEstimate(
            flops=0, bytes_accessed=4 * math.prod(shape), transcendentals=0
        ),
    )(*in_hbm(source))


def load_in(w_in, first, tiles):
    units = w_in.shape[0]
    kernel = functools.partial(load_in_kernel, first)
    loaded = load(kernel, w_in, (tiles, units, 2, LANES), tiles)
    return loaded.reshape(tiles, 2 * units, LANES)


def expert_kernel(exp_dev, experts, count, *refs):
    group_ref = refs[0]
    x_refs = refs[1 : 1 + count]
    low_ref, high_ref, wout_ref, send_ref, keep_ref, mixed, hidden = refs[1 + count :]
    lines = low_ref.shape[1]
    width = wout_ref.shape[1]
    per = lines // exp_dev
    rows = sum(ref.shape[0] for ref in x_refs)
    x = jnp.concatenate([ref[:, :width] for ref in x_refs], axis=0)
    tail = jnp.concatenate([ref[:, width:] for ref in x_refs], axis=0)
    contract_last = (((1,), (1,)), ((), ()))
    column = lax.broadcasted_iota(jnp.int32, (16, tail.shape[1]), 1)
    wanted = lax.broadcasted_iota(jnp.int32, (16, tail.shape[1]), 0) + group_ref[0] * exp_dev
    select = (column % experts == wanted) & (column < 3 * experts)
    scale = lax.dot_general(
        select.astype(jnp.bfloat16), tail, contract_last, preferred_element_type=jnp.float32
    )
    for e in range(exp_dev):
        w = jnp.concatenate(
            [
                ref[t, pl.ds(e * per, per), :]
                for ref in (low_ref, high_ref)
                for t in range(ref.shape[0])
            ],
            axis=1,
        )
        both = lax.dot_general(w, x, contract_last, preferred_element_type=jnp.float32)
        for r in range(0, rows, LANES):
            mixed[...] = both[:, r : r + LANES]
            gate = mixed[pl.ds(0, per // 2, stride=2), :]
            up = mixed[pl.ds(1, per // 2, stride=2), :]
            act = gate / (1.0 + jnp.exp(-gate)) * up * scale[e : e + 1, r : r + LANES]
            hidden[pl.ds(e * per // 2, per // 2), r : r + LANES] = act.astype(jnp.bfloat16)
    chunk = min(512, width)
    pieces, piece, _ = keep_ref.shape
    for c in range(0, width, chunk):
        part = lax.dot_general(
            hidden[...],
            wout_ref[:, c : c + chunk],
            (((0,), (0,)), ((), ())),
            preferred_element_type=jnp.float32,
        )
        for p in range(pieces):
            keep_ref[p, :, c : c + chunk] = part[p * piece : (p + 1) * piece]
            other = part[(pieces + p) * piece : (pieces + p + 1) * piece]
            send_ref[p, :, c : c + chunk] = other.astype(jnp.bfloat16)


def run_experts(group, blocks, low, high, wout, exp_dev, experts):
    packed_width = blocks[0].shape[1]
    half_rows = sum(block.shape[0] for block in blocks) // 2
    count = len(blocks)
    width = wout.shape[1]
    lines = low.shape[1]
    one_step = half_rows <= LANES
    if one_step:
        x_block, out_block, grid = VMEM, VMEM, ()
        pieces, piece, rows = 1, half_rows, 2 * half_rows
        windows = 0
    else:
        pieces, piece, block = count // 2, blocks[0].shape[0], 16
        x_block = pl.BlockSpec((block, packed_width), lambda i: (i, 0))
        out_block = pl.BlockSpec((pieces, block, width), lambda i: (0, i, 0))
        grid = (piece // block,)
        rows = count * block
        windows = 2 * rows * (2 * packed_width + 3 * width)
    scratch = rows * (6 * lines + 6 * width)
    send, keep = pl.pallas_call(
        functools.partial(expert_kernel, exp_dev, experts, count),
        grid=grid,
        out_shape=(
            jax.ShapeDtypeStruct((pieces, piece, width), jnp.bfloat16),
            jax.ShapeDtypeStruct((pieces, piece, width), jnp.float32),
        ),
        in_specs=[pl.BlockSpec(memory_space=pltpu.SMEM), *[x_block] * count, VMEM, VMEM, VMEM],
        out_specs=[out_block, out_block],
        scratch_shapes=[
            pltpu.VMEM((lines // exp_dev, LANES), jnp.float32),
            pltpu.VMEM((lines // 2, rows), jnp.bfloat16),
        ],
        compiler_params=pltpu.CompilerParams(vmem_limit_bytes=windows + scratch + 4 * MIB),
        cost_estimate=pl.CostEstimate(
            flops=6 * half_rows * width * lines,
            bytes_accessed=4 * half_rows * packed_width + 6 * half_rows * width,
            transcendentals=half_rows * lines,
        ),
    )(group, *blocks, *in_vmem(low, high, wout))
    return send.reshape(half_rows, width), keep.reshape(half_rows, width)


def halve(rows, stride):
    size = rows.shape[0] // 2
    sent = rows[size:].astype(jnp.bfloat16)
    return rows[:size] + swap(sent, "expert", stride).astype(jnp.float32)


def body(tokens, expert_ids, route_weights, in_weights, out_weights):
    width = tokens.shape[1]
    exp_dev, units = in_weights.shape[:2]
    groups = lax.axis_size("expert")
    planes = lax.axis_size("batch")
    experts = exp_dev * groups
    far = planes - 1
    strides = [groups >> i for i in range(1, groups.bit_length() - 1)]
    w_in = in_weights.reshape(exp_dev * units, 2, width)
    w_out = out_weights.reshape(exp_dev * units, width)

    group = lax.axis_index("expert").astype(jnp.int32).reshape(1)
    x = pack(tokens, expert_ids, route_weights, experts)
    x, group, w_in, w_out = lax.optimization_barrier((x, group, w_in, w_out))
    tiles = width // LANES
    wout = load(load_out_kernel, w_out, w_out.shape, 8)
    for stride in strides[:-1]:
        x, wout = stack(x, swap(x, "expert", stride), [wout])
    x, w_in = lax.optimization_barrier((x, w_in))
    across = swap(x, "batch", far)
    mine = swap(x, "expert", strides[-1])
    low = load_in(w_in, 0, tiles // 2)
    across, mine, low = lax.optimization_barrier((across, mine, low))
    mine, wout, low = stack(x, mine, [wout, low])
    mine, across, w_in = lax.optimization_barrier((mine, across, w_in))
    early = [mine, across]
    late = [swap(mine, "batch", b) for b in range(1, far)]
    late.append(swap(across, "expert", strides[-1]))
    early_core = [swap(block, "expert", 1) for block in early]
    high = load_in(w_in, tiles // 2, tiles - tiles // 2)
    late, high = lax.optimization_barrier((late, high))
    late_core = [swap(block, "expert", 1) for block in late]
    blocks = []
    for (mine, across), rest in ((early, late), (early_core, late_core)):
        if 2 * mine.shape[0] * planes <= 2 * LANES:
            blocks += [mine] + rest[:-1] + [across, rest[-1]]
        else:
            blocks += [mine] + rest[:-1] + [jnp.concatenate([across, rest[-1]], axis=0)]

    send, total = run_experts(group, blocks, low, high, wout, exp_dev, experts)
    total = total + swap(send, "expert", 1).astype(jnp.float32)
    size = total.shape[0] // planes
    rounded = total.astype(jnp.bfloat16)
    mine = total[:size]
    for b in range(1, far):
        piece = rounded[b * size : (b + 1) * size]
        mine = mine + swap(piece, "batch", b).astype(jnp.float32)
    across = total[far * size :]
    for stride in reversed(strides):
        across = halve(across, stride)
    across = swap(across.astype(jnp.bfloat16), "batch", far).astype(jnp.float32)
    for stride in reversed(strides):
        mine = halve(mine, stride)
    mine = mine + across
    return mine.astype(jnp.bfloat16)


def solution(mesh):
    return jax.shard_map(
        body,
        mesh=mesh,
        in_specs=(
            P(("batch", "expert"), None),
            P(("batch", "expert"), None),
            P(("batch", "expert"), None),
            P("expert", "batch", None, None),
            P("expert", "batch", None),
        ),
        out_specs=P(("batch", "expert"), None),
        check_vma=False,
    )
```

```python
import functools
import math

import jax
import jax.numpy as jnp
from jax import lax
from jax.experimental import pallas as pl
from jax.experimental.pallas import tpu as pltpu
from jax.sharding import PartitionSpec as P

LANES = 128
MIB = 1 << 20
VMEM = pl.BlockSpec(memory_space=pltpu.VMEM)
HBM = pl.BlockSpec(memory_space=pltpu.HBM)


def in_hbm(*arrays):
    return [pltpu.with_memory_space_constraint(array, pltpu.HBM) for array in arrays]


def in_vmem(*arrays):
    return [pltpu.with_memory_space_constraint(array, pltpu.VMEM) for array in arrays]


def swap(block, axis, flips):
    size = lax.axis_size(axis)
    return lax.ppermute(block, axis, [(i, i ^ flips) for i in range(size)])


def pack_kernel(
    experts, tokens_hbm, ids_hbm, weights_hbm, packed_ref, tokens_ref, ids_ref, weights_ref, sems
):
    copies = [
        pltpu.make_async_copy(source, target, sems.at[i])
        for i, (source, target) in enumerate(
            ((ids_hbm, ids_ref), (weights_hbm, weights_ref), (tokens_hbm, tokens_ref))
        )
    ]
    for copy in copies:
        copy.start()
    for copy in copies:
        copy.wait()
    rows, width = tokens_ref.shape
    tail = packed_ref.shape[1] - width
    packed_ref[:, :width] = tokens_ref[...]
    lane = lax.broadcasted_iota(jnp.int32, (rows, tail), 1)
    expert = lane % experts
    part = lane // experts
    dense = jnp.zeros((rows, tail), jnp.float32)
    for k in range(ids_ref.shape[1]):
        dense += jnp.where(ids_ref[:, k : k + 1] == expert, weights_ref[:, k : k + 1], 0.0)
    result = jnp.zeros((rows, tail), jnp.float32)
    for step in range(3):
        rounded = dense.astype(jnp.bfloat16).astype(jnp.float32)
        result = jnp.where(part == step, rounded, result)
        dense = dense - rounded
    packed_ref[:, width:] = result.astype(jnp.bfloat16)


def pack(tokens, expert_ids, route_weights, experts):
    rows, width = tokens.shape
    tail = -(-3 * experts // LANES) * LANES
    return pl.pallas_call(
        functools.partial(pack_kernel, experts),
        out_shape=jax.ShapeDtypeStruct((rows, width + tail), jnp.bfloat16),
        in_specs=[HBM] * 3,
        out_specs=VMEM,
        scratch_shapes=[
            pltpu.VMEM(tokens.shape, tokens.dtype),
            pltpu.VMEM(expert_ids.shape, expert_ids.dtype),
            pltpu.VMEM(route_weights.shape, route_weights.dtype),
            pltpu.SemaphoreType.DMA((3,)),
        ],
        compiler_params=pltpu.CompilerParams(vmem_limit_bytes=2 * MIB),
    )(*in_hbm(tokens, expert_ids, route_weights))


def stack_kernel(count, first_ref, second_ref, *refs):
    out_ref = refs[count]
    rows = first_ref.shape[0]
    out_ref[:rows, :] = first_ref[...]
    out_ref[rows:, :] = second_ref[...]


def stack(first, second, held):
    rows, width = first.shape
    return pl.pallas_call(
        functools.partial(stack_kernel, len(held)),
        out_shape=[jax.ShapeDtypeStruct((rows + second.shape[0], width), first.dtype)]
        + [pltpu.VMEM(array.shape, array.dtype) for array in held],
        in_specs=[VMEM] * (2 + len(held)),
        out_specs=[VMEM] * (1 + len(held)),
        input_output_aliases={2 + i: 1 + i for i in range(len(held))},
        compiler_params=pltpu.CompilerParams(vmem_limit_bytes=2 * MIB),
    )(first, second, *in_vmem(*held))


def load_in_kernel(first, in_ref, in_vmem, sems):
    copies = [
        pltpu.make_async_copy(
            in_ref.at[:, :, pl.ds((first + t) * LANES, LANES)], in_vmem.at[t], sems.at[t]
        )
        for t in range(in_vmem.shape[0])
    ]
    for copy in copies:
        copy.start()
    for copy in copies:
        copy.wait()


def load_out_kernel(out_ref, out_vmem, sems):
    copies = []
    step = out_ref.shape[0] // sems.shape[0]
    for i in range(sems.shape[0]):
        rows = pl.ds(i * step, step)
        copies.append(pltpu.make_async_copy(out_ref.at[rows], out_vmem.at[rows], sems.at[i]))
    for copy in copies:
        copy.start()
    for copy in copies:
        copy.wait()


def load(kernel, source, shape, copies):
    return pl.pallas_call(
        kernel,
        out_shape=pltpu.VMEM(shape, source.dtype),
        in_specs=[HBM],
        out_specs=VMEM,
        scratch_shapes=[pltpu.SemaphoreType.DMA((copies,))],
        compiler_params=pltpu.CompilerParams(vmem_limit_bytes=2 * MIB),
        cost_estimate=pl.CostEstimate(
            flops=0, bytes_accessed=4 * math.prod(shape), transcendentals=0
        ),
    )(*in_hbm(source))


def load_in(w_in, first, tiles):
    units = w_in.shape[0]
    kernel = functools.partial(load_in_kernel, first)
    loaded = load(kernel, w_in, (tiles, units, 2, LANES), tiles)
    return loaded.reshape(tiles, 2 * units, LANES)


def expert_kernel(exp_dev, experts, count, *refs):
    group_ref = refs[0]
    x_refs = refs[1 : 1 + count]
    low_ref, high_ref, wout_ref = refs[1 + count : 4 + count]
    send_refs, keep_refs = refs[4 + count : 6 + count], refs[6 + count : 8 + count]
    mixed, hidden = refs[8 + count :]
    lines = low_ref.shape[1]
    width = wout_ref.shape[1]
    per = lines // exp_dev
    rows = sum(ref.shape[0] for ref in x_refs)
    x = jnp.concatenate([ref[:, :width] for ref in x_refs], axis=0)
    tail = jnp.concatenate([ref[:, width:] for ref in x_refs], axis=0)
    contract_last = (((1,), (1,)), ((), ()))
    column = lax.broadcasted_iota(jnp.int32, (16, tail.shape[1]), 1)
    wanted = lax.broadcasted_iota(jnp.int32, (16, tail.shape[1]), 0) + group_ref[0] * exp_dev
    select = (column % experts == wanted) & (column < 3 * experts)
    scale = lax.dot_general(
        select.astype(jnp.bfloat16), tail, contract_last, preferred_element_type=jnp.float32
    )
    for e in range(exp_dev):
        w = jnp.concatenate(
            [
                ref[t, pl.ds(e * per, per), :]
                for ref in (low_ref, high_ref)
                for t in range(ref.shape[0])
            ],
            axis=1,
        )
        both = lax.dot_general(w, x, contract_last, preferred_element_type=jnp.float32)
        for r in range(0, rows, LANES):
            mixed[...] = both[:, r : r + LANES]
            gate = mixed[pl.ds(0, per // 2, stride=2), :]
            up = mixed[pl.ds(1, per // 2, stride=2), :]
            act = gate / (1.0 + jnp.exp(-gate)) * up * scale[e : e + 1, r : r + LANES]
            hidden[pl.ds(e * per // 2, per // 2), r : r + LANES] = act.astype(jnp.bfloat16)
    chunk = min(512, width)
    ahead, piece, _ = keep_refs[0].shape
    pieces = ahead + keep_refs[1].shape[0]
    for c in range(0, width, chunk):
        part = lax.dot_general(
            hidden[...],
            wout_ref[:, c : c + chunk],
            (((0,), (0,)), ((), ())),
            preferred_element_type=jnp.float32,
        )
        for p in range(2 * pieces):
            targets = keep_refs if p < pieces else send_refs
            q = p % pieces
            target = targets[0].at[q] if q < ahead else targets[1].at[q - ahead]
            target[:, c : c + chunk] = part[p * piece : (p + 1) * piece].astype(target.dtype)


def run_experts(group, blocks, pieces, low, high, wout, exp_dev, experts):
    packed_width = blocks[0].shape[1]
    half_rows = sum(block.shape[0] for block in blocks) // 2
    piece = half_rows // pieces
    ahead = pieces - 2
    count = len(blocks)
    width = wout.shape[1]
    lines = low.shape[1]
    if half_rows <= LANES:
        x_block, out_blocks, grid = VMEM, [VMEM] * 4, ()
        rows, windows = 2 * half_rows, 0
    else:
        block = 16
        x_block = pl.BlockSpec((block, packed_width), lambda i: (i, 0))
        out_blocks = [
            pl.BlockSpec((n, block, width), lambda i: (0, i, 0)) for n in (ahead, 2, ahead, 2)
        ]
        grid = (piece // block,)
        rows = count * block
        windows = 2 * rows * (2 * packed_width + 3 * width)
    scratch = rows * (6 * lines + 6 * width)
    return pl.pallas_call(
        functools.partial(expert_kernel, exp_dev, experts, count),
        grid=grid,
        out_shape=(
            jax.ShapeDtypeStruct((ahead, piece, width), jnp.bfloat16),
            jax.ShapeDtypeStruct((2, piece, width), jnp.bfloat16),
            jax.ShapeDtypeStruct((ahead, piece, width), jnp.float32),
            jax.ShapeDtypeStruct((2, piece, width), jnp.float32),
        ),
        in_specs=[pl.BlockSpec(memory_space=pltpu.SMEM), *[x_block] * count, VMEM, VMEM, VMEM],
        out_specs=out_blocks,
        scratch_shapes=[
            pltpu.VMEM((lines // exp_dev, LANES), jnp.float32),
            pltpu.VMEM((lines // 2, rows), jnp.bfloat16),
        ],
        compiler_params=pltpu.CompilerParams(vmem_limit_bytes=windows + scratch + 4 * MIB),
        cost_estimate=pl.CostEstimate(
            flops=6 * half_rows * width * lines,
            bytes_accessed=4 * half_rows * packed_width + 6 * half_rows * width,
            transcendentals=half_rows * lines,
        ),
    )(group, *blocks, *in_vmem(low, high, wout))


def halve(rows, stride):
    size = rows.shape[0] // 2
    sent = rows[size:].astype(jnp.bfloat16)
    return rows[:size] + swap(sent, "expert", stride).astype(jnp.float32)


def body(tokens, expert_ids, route_weights, in_weights, out_weights):
    width = tokens.shape[1]
    exp_dev, units = in_weights.shape[:2]
    groups = lax.axis_size("expert")
    planes = lax.axis_size("batch")
    experts = exp_dev * groups
    far = planes - 1
    strides = [groups >> i for i in range(1, groups.bit_length() - 1)]
    w_in = in_weights.reshape(exp_dev * units, 2, width)
    w_out = out_weights.reshape(exp_dev * units, width)

    group = lax.axis_index("expert").astype(jnp.int32).reshape(1)
    x = pack(tokens, expert_ids, route_weights, experts)
    x, group, w_in, w_out = lax.optimization_barrier((x, group, w_in, w_out))
    tiles = width // LANES
    wout = load(load_out_kernel, w_out, w_out.shape, 8)
    for stride in strides[:-1]:
        x, wout = stack(x, swap(x, "expert", stride), [wout])
    x, w_in = lax.optimization_barrier((x, w_in))
    across = swap(x, "batch", far)
    mine = swap(x, "expert", strides[-1])
    low = load_in(w_in, 0, tiles // 2)
    across, mine, low = lax.optimization_barrier((across, mine, low))
    mine, wout, low = stack(x, mine, [wout, low])
    mine, across, w_in = lax.optimization_barrier((mine, across, w_in))
    early = [mine, across]
    late = [swap(mine, "batch", b) for b in range(1, far)]
    late.append(swap(across, "expert", strides[-1]))
    early_core = [swap(block, "expert", 1) for block in early]
    high = load_in(w_in, tiles // 2, tiles - tiles // 2)
    late, high = lax.optimization_barrier((late, high))
    late_core = [swap(block, "expert", 1) for block in late]
    blocks = []
    for (mine, across), rest in ((early, late), (early_core, late_core)):
        if mine.shape[0] * planes <= LANES:
            blocks += rest[:-1] + [mine, across, rest[-1]]
        else:
            blocks += rest[:-1] + [mine, jnp.concatenate([across, rest[-1]], axis=0)]

    sends = run_experts(group, blocks, planes, low, high, wout, exp_dev, experts)
    first, second, kept, total = sends
    arrived, second = lax.optimization_barrier((swap(first, "expert", 1), second))
    first = (kept + arrived.astype(jnp.float32)).astype(jnp.bfloat16)
    moved = [swap(first[b - 1], "batch", b) for b in range(1, far)]
    total = total + swap(second, "expert", 1).astype(jnp.float32)
    mine, across = total[0], total[1]
    for rows in moved:
        mine = mine + rows.astype(jnp.float32)
    for stride in reversed(strides):
        across = halve(across, stride)
    across = swap(across.astype(jnp.bfloat16), "batch", far).astype(jnp.float32)
    for stride in reversed(strides):
        mine = halve(mine, stride)
    mine = mine + across
    return mine.astype(jnp.bfloat16)


def solution(mesh):
    return jax.shard_map(
        body,
        mesh=mesh,
        in_specs=(
            P(("batch", "expert"), None),
            P(("batch", "expert"), None),
            P(("batch", "expert"), None),
            P("expert", "batch", None, None),
            P("expert", "batch", None),
        ),
        out_specs=P(("batch", "expert"), None),
        check_vma=False,
    )
```

```python
import functools
import math

import jax
import jax.numpy as jnp
from jax import lax
from jax.experimental import pallas as pl
from jax.experimental.pallas import tpu as pltpu
from jax.sharding import PartitionSpec as P

LANES = 128
MIB = 1 << 20
VMEM = pl.BlockSpec(memory_space=pltpu.VMEM)
HBM = pl.BlockSpec(memory_space=pltpu.HBM)


def in_hbm(*arrays):
    return [pltpu.with_memory_space_constraint(array, pltpu.HBM) for array in arrays]


def in_vmem(*arrays):
    return [pltpu.with_memory_space_constraint(array, pltpu.VMEM) for array in arrays]


def swap(block, axis, flips):
    size = lax.axis_size(axis)
    return lax.ppermute(block, axis, [(i, i ^ flips) for i in range(size)])


def pack_kernel(
    experts, tokens_hbm, ids_hbm, weights_hbm, packed_ref, tokens_ref, ids_ref, weights_ref, sems
):
    copies = [
        pltpu.make_async_copy(source, target, sems.at[i])
        for i, (source, target) in enumerate(
            ((ids_hbm, ids_ref), (weights_hbm, weights_ref), (tokens_hbm, tokens_ref))
        )
    ]
    for copy in copies:
        copy.start()
    for copy in copies:
        copy.wait()
    rows, width = tokens_ref.shape
    tail = packed_ref.shape[1] - width
    packed_ref[:, :width] = tokens_ref[...]
    lane = lax.broadcasted_iota(jnp.int32, (rows, tail), 1)
    expert = lane % experts
    part = lane // experts
    dense = jnp.zeros((rows, tail), jnp.float32)
    for k in range(ids_ref.shape[1]):
        dense += jnp.where(ids_ref[:, k : k + 1] == expert, weights_ref[:, k : k + 1], 0.0)
    result = jnp.zeros((rows, tail), jnp.float32)
    for step in range(3):
        rounded = dense.astype(jnp.bfloat16).astype(jnp.float32)
        result = jnp.where(part == step, rounded, result)
        dense = dense - rounded
    packed_ref[:, width:] = result.astype(jnp.bfloat16)


def pack(tokens, expert_ids, route_weights, experts):
    rows, width = tokens.shape
    tail = -(-3 * experts // LANES) * LANES
    return pl.pallas_call(
        functools.partial(pack_kernel, experts),
        out_shape=jax.ShapeDtypeStruct((rows, width + tail), jnp.bfloat16),
        in_specs=[HBM] * 3,
        out_specs=VMEM,
        scratch_shapes=[
            pltpu.VMEM(tokens.shape, tokens.dtype),
            pltpu.VMEM(expert_ids.shape, expert_ids.dtype),
            pltpu.VMEM(route_weights.shape, route_weights.dtype),
            pltpu.SemaphoreType.DMA((3,)),
        ],
        compiler_params=pltpu.CompilerParams(vmem_limit_bytes=2 * MIB),
    )(*in_hbm(tokens, expert_ids, route_weights))


def stack_kernel(count, first_ref, second_ref, *refs):
    out_ref = refs[count]
    rows = first_ref.shape[0]
    out_ref[:rows, :] = first_ref[...]
    out_ref[rows:, :] = second_ref[...]


def stack(first, second, held):
    rows, width = first.shape
    return pl.pallas_call(
        functools.partial(stack_kernel, len(held)),
        out_shape=[jax.ShapeDtypeStruct((rows + second.shape[0], width), first.dtype)]
        + [pltpu.VMEM(array.shape, array.dtype) for array in held],
        in_specs=[VMEM] * (2 + len(held)),
        out_specs=[VMEM] * (1 + len(held)),
        input_output_aliases={2 + i: 1 + i for i in range(len(held))},
        compiler_params=pltpu.CompilerParams(vmem_limit_bytes=2 * MIB),
    )(first, second, *in_vmem(*held))


def load_in_kernel(first, in_ref, in_vmem, sems):
    copies = [
        pltpu.make_async_copy(
            in_ref.at[:, :, pl.ds((first + t) * LANES, LANES)], in_vmem.at[t], sems.at[t]
        )
        for t in range(in_vmem.shape[0])
    ]
    for copy in copies:
        copy.start()
    for copy in copies:
        copy.wait()


def load_out_kernel(out_ref, out_vmem, sems):
    copies = []
    step = out_ref.shape[0] // sems.shape[0]
    for i in range(sems.shape[0]):
        rows = pl.ds(i * step, step)
        copies.append(pltpu.make_async_copy(out_ref.at[rows], out_vmem.at[rows], sems.at[i]))
    for copy in copies:
        copy.start()
    for copy in copies:
        copy.wait()


def load(kernel, source, shape, copies):
    return pl.pallas_call(
        kernel,
        out_shape=pltpu.VMEM(shape, source.dtype),
        in_specs=[HBM],
        out_specs=VMEM,
        scratch_shapes=[pltpu.SemaphoreType.DMA((copies,))],
        compiler_params=pltpu.CompilerParams(vmem_limit_bytes=2 * MIB),
        cost_estimate=pl.CostEstimate(
            flops=0, bytes_accessed=4 * math.prod(shape), transcendentals=0
        ),
    )(*in_hbm(source))


def load_in(w_in, first, tiles):
    units = w_in.shape[0]
    kernel = functools.partial(load_in_kernel, first)
    loaded = load(kernel, w_in, (tiles, units, 2, LANES), tiles)
    return loaded.reshape(tiles, 2 * units, LANES)


def expert_kernel(exp_dev, experts, count, *refs):
    group_ref = refs[0]
    x_refs = refs[1 : 1 + count]
    low_ref, high_ref, wout_ref = refs[1 + count : 4 + count]
    send_refs, keep_refs = refs[4 + count : 6 + count], refs[6 + count : 8 + count]
    mixed, hidden = refs[8 + count :]
    lines = low_ref.shape[1]
    width = wout_ref.shape[1]
    per = lines // exp_dev
    rows = sum(ref.shape[0] for ref in x_refs)
    x = jnp.concatenate([ref[:, :width] for ref in x_refs], axis=0)
    tail = jnp.concatenate([ref[:, width:] for ref in x_refs], axis=0)
    contract_last = (((1,), (1,)), ((), ()))
    column = lax.broadcasted_iota(jnp.int32, (16, tail.shape[1]), 1)
    wanted = lax.broadcasted_iota(jnp.int32, (16, tail.shape[1]), 0) + group_ref[0] * exp_dev
    select = (column % experts == wanted) & (column < 3 * experts)
    scale = lax.dot_general(
        select.astype(jnp.bfloat16), tail, contract_last, preferred_element_type=jnp.float32
    )
    for e in range(exp_dev):
        w = jnp.concatenate(
            [
                ref[t, pl.ds(e * per, per), :]
                for ref in (low_ref, high_ref)
                for t in range(ref.shape[0])
            ],
            axis=1,
        )
        both = lax.dot_general(w, x, contract_last, preferred_element_type=jnp.float32)
        for r in range(0, rows, LANES):
            mixed[...] = both[:, r : r + LANES]
            gate = mixed[pl.ds(0, per // 2, stride=2), :]
            up = mixed[pl.ds(1, per // 2, stride=2), :]
            act = gate / (1.0 + jnp.exp(-gate)) * up * scale[e : e + 1, r : r + LANES]
            hidden[pl.ds(e * per // 2, per // 2), r : r + LANES] = act.astype(jnp.bfloat16)
    chunk = min(512, width)
    ahead, piece, _ = keep_refs[0].shape
    pieces = ahead + keep_refs[1].shape[0]
    for c in range(0, width, chunk):
        part = lax.dot_general(
            hidden[...],
            wout_ref[:, c : c + chunk],
            (((0,), (0,)), ((), ())),
            preferred_element_type=jnp.float32,
        )
        for p in range(2 * pieces):
            targets = keep_refs if p < pieces else send_refs
            q = p % pieces
            target = targets[0].at[q] if q < ahead else targets[1].at[q - ahead]
            target[:, c : c + chunk] = part[p * piece : (p + 1) * piece].astype(target.dtype)


def run_experts(group, blocks, pieces, low, high, wout, exp_dev, experts):
    packed_width = blocks[0].shape[1]
    half_rows = sum(block.shape[0] for block in blocks) // 2
    piece = half_rows // pieces
    ahead = pieces - 2
    count = len(blocks)
    width = wout.shape[1]
    lines = low.shape[1]
    if half_rows <= LANES:
        x_block, out_blocks, grid = VMEM, [VMEM] * 4, ()
        rows, windows = 2 * half_rows, 0
    else:
        block = 16
        x_block = pl.BlockSpec((block, packed_width), lambda i: (i, 0))
        out_blocks = [
            pl.BlockSpec((n, block, width), lambda i: (0, i, 0)) for n in (ahead, 2, ahead, 2)
        ]
        grid = (piece // block,)
        rows = count * block
        windows = 2 * rows * (2 * packed_width + 3 * width)
    scratch = rows * (6 * lines + 6 * width)
    return pl.pallas_call(
        functools.partial(expert_kernel, exp_dev, experts, count),
        grid=grid,
        out_shape=(
            jax.ShapeDtypeStruct((ahead, piece, width), jnp.bfloat16),
            jax.ShapeDtypeStruct((2, piece, width), jnp.bfloat16),
            jax.ShapeDtypeStruct((ahead, piece, width), jnp.float32),
            jax.ShapeDtypeStruct((2, piece, width), jnp.float32),
        ),
        in_specs=[pl.BlockSpec(memory_space=pltpu.SMEM), *[x_block] * count, VMEM, VMEM, VMEM],
        out_specs=out_blocks,
        scratch_shapes=[
            pltpu.VMEM((lines // exp_dev, LANES), jnp.float32),
            pltpu.VMEM((lines // 2, rows), jnp.bfloat16),
        ],
        compiler_params=pltpu.CompilerParams(vmem_limit_bytes=windows + scratch + 4 * MIB),
        cost_estimate=pl.CostEstimate(
            flops=6 * half_rows * width * lines,
            bytes_accessed=4 * half_rows * packed_width + 6 * half_rows * width,
            transcendentals=half_rows * lines,
        ),
    )(group, *blocks, *in_vmem(low, high, wout))


def halve(rows, stride):
    size = rows.shape[0] // 2
    sent = rows[size:].astype(jnp.bfloat16)
    return rows[:size] + swap(sent, "expert", stride).astype(jnp.float32)


def body(tokens, expert_ids, route_weights, in_weights, out_weights):
    width = tokens.shape[1]
    exp_dev, units = in_weights.shape[:2]
    groups = lax.axis_size("expert")
    planes = lax.axis_size("batch")
    experts = exp_dev * groups
    far = planes - 1
    strides = [groups >> i for i in range(1, groups.bit_length() - 1)]
    w_in = in_weights.reshape(exp_dev * units, 2, width)
    w_out = out_weights.reshape(exp_dev * units, width)

    group = lax.axis_index("expert").astype(jnp.int32).reshape(1)
    x = pack(tokens, expert_ids, route_weights, experts)
    x, group, w_in, w_out = lax.optimization_barrier((x, group, w_in, w_out))
    tiles = width // LANES
    wout = load(load_out_kernel, w_out, w_out.shape, 8)
    for stride in strides[:-1]:
        x, wout = stack(x, swap(x, "expert", stride), [wout])
    x, w_in = lax.optimization_barrier((x, w_in))
    across = swap(x, "batch", far)
    mine = swap(x, "expert", strides[-1])
    low = load_in(w_in, 0, tiles // 2)
    across, mine, low = lax.optimization_barrier((across, mine, low))
    mine, wout, low = stack(x, mine, [wout, low])
    mine, across, w_in = lax.optimization_barrier((mine, across, w_in))
    early = [mine, across]
    late = [swap(mine, "batch", b) for b in range(1, far)]
    late.append(swap(across, "expert", strides[-1]))
    early_core = [swap(block, "expert", 1) for block in early]
    high = load_in(w_in, tiles // 2, tiles - tiles // 2)
    late, high = lax.optimization_barrier((late, high))
    late_core = [swap(block, "expert", 1) for block in late]
    blocks = []
    for (mine, across), rest in ((early, late), (early_core, late_core)):
        if mine.shape[0] * planes <= LANES:
            blocks += rest[:-1] + [mine, across, rest[-1]]
        else:
            blocks += rest[:-1] + [mine, jnp.concatenate([across, rest[-1]], axis=0)]

    sends = run_experts(group, blocks, planes, low, high, wout, exp_dev, experts)
    first, second, kept, total = sends
    arrived, second = lax.optimization_barrier((swap(first, "expert", 1), second))
    first = (kept + arrived.astype(jnp.float32)).astype(jnp.bfloat16)
    moved = [swap(first[b - 1], "batch", b) for b in range(1, far)]
    total = total + swap(second, "expert", 1).astype(jnp.float32)
    mine, across = total[0], total[1]
    for rows in moved:
        mine = mine + rows.astype(jnp.float32)
    across = halve(across, strides[-1])
    mine = halve(mine, strides[-1])
    mine = mine + swap(across.astype(jnp.bfloat16), "batch", far).astype(jnp.float32)
    for stride in reversed(strides[:-1]):
        mine = halve(mine, stride)
    return mine.astype(jnp.bfloat16)


def solution(mesh):
    return jax.shard_map(
        body,
        mesh=mesh,
        in_specs=(
            P(("batch", "expert"), None),
            P(("batch", "expert"), None),
            P(("batch", "expert"), None),
            P("expert", "batch", None, None),
            P("expert", "batch", None),
        ),
        out_specs=P(("batch", "expert"), None),
        check_vma=False,
    )
```

```python
import functools
import math

import jax
import jax.numpy as jnp
from jax import lax
from jax.experimental import pallas as pl
from jax.experimental.pallas import tpu as pltpu
from jax.sharding import PartitionSpec as P

LANES = 128
MIB = 1 << 20
VMEM = pl.BlockSpec(memory_space=pltpu.VMEM)
HBM = pl.BlockSpec(memory_space=pltpu.HBM)


def in_hbm(*arrays):
    return [pltpu.with_memory_space_constraint(array, pltpu.HBM) for array in arrays]


def in_vmem(*arrays):
    return [pltpu.with_memory_space_constraint(array, pltpu.VMEM) for array in arrays]


def swap(block, axis, flips):
    size = lax.axis_size(axis)
    return lax.ppermute(block, axis, [(i, i ^ flips) for i in range(size)])


def pack_kernel(
    experts, tokens_hbm, ids_hbm, weights_hbm, packed_ref, tokens_ref, ids_ref, weights_ref, sems
):
    copies = [
        pltpu.make_async_copy(source, target, sems.at[i])
        for i, (source, target) in enumerate(
            ((ids_hbm, ids_ref), (weights_hbm, weights_ref), (tokens_hbm, tokens_ref))
        )
    ]
    for copy in copies:
        copy.start()
    for copy in copies:
        copy.wait()
    rows, width = tokens_ref.shape
    tail = packed_ref.shape[1] - width
    packed_ref[:, :width] = tokens_ref[...]
    lane = lax.broadcasted_iota(jnp.int32, (rows, tail), 1)
    expert = lane % experts
    part = lane // experts
    dense = jnp.zeros((rows, tail), jnp.float32)
    for k in range(ids_ref.shape[1]):
        dense += jnp.where(ids_ref[:, k : k + 1] == expert, weights_ref[:, k : k + 1], 0.0)
    result = jnp.zeros((rows, tail), jnp.float32)
    for step in range(3):
        rounded = dense.astype(jnp.bfloat16).astype(jnp.float32)
        result = jnp.where(part == step, rounded, result)
        dense = dense - rounded
    packed_ref[:, width:] = result.astype(jnp.bfloat16)


def pack(tokens, expert_ids, route_weights, experts):
    rows, width = tokens.shape
    tail = -(-3 * experts // LANES) * LANES
    return pl.pallas_call(
        functools.partial(pack_kernel, experts),
        out_shape=jax.ShapeDtypeStruct((rows, width + tail), jnp.bfloat16),
        in_specs=[HBM] * 3,
        out_specs=VMEM,
        scratch_shapes=[
            pltpu.VMEM(tokens.shape, tokens.dtype),
            pltpu.VMEM(expert_ids.shape, expert_ids.dtype),
            pltpu.VMEM(route_weights.shape, route_weights.dtype),
            pltpu.SemaphoreType.DMA((3,)),
        ],
        compiler_params=pltpu.CompilerParams(vmem_limit_bytes=2 * MIB),
    )(*in_hbm(tokens, expert_ids, route_weights))


def stack_kernel(count, first_ref, second_ref, *refs):
    out_ref = refs[count]
    rows = first_ref.shape[0]
    out_ref[:rows, :] = first_ref[...]
    out_ref[rows:, :] = second_ref[...]


def stack(first, second, held):
    rows, width = first.shape
    return pl.pallas_call(
        functools.partial(stack_kernel, len(held)),
        out_shape=[jax.ShapeDtypeStruct((rows + second.shape[0], width), first.dtype)]
        + [pltpu.VMEM(array.shape, array.dtype) for array in held],
        in_specs=[VMEM] * (2 + len(held)),
        out_specs=[VMEM] * (1 + len(held)),
        input_output_aliases={2 + i: 1 + i for i in range(len(held))},
        compiler_params=pltpu.CompilerParams(vmem_limit_bytes=2 * MIB),
    )(first, second, *in_vmem(*held))


def load_in_kernel(first, in_ref, in_vmem, sems):
    copies = [
        pltpu.make_async_copy(
            in_ref.at[:, :, pl.ds((first + t) * LANES, LANES)], in_vmem.at[t], sems.at[t]
        )
        for t in range(in_vmem.shape[0])
    ]
    for copy in copies:
        copy.start()
    for copy in copies:
        copy.wait()


def load_out_kernel(out_ref, out_vmem, sems):
    copies = []
    step = out_ref.shape[0] // sems.shape[0]
    for i in range(sems.shape[0]):
        rows = pl.ds(i * step, step)
        copies.append(pltpu.make_async_copy(out_ref.at[rows], out_vmem.at[rows], sems.at[i]))
    for copy in copies:
        copy.start()
    for copy in copies:
        copy.wait()


def load(kernel, source, shape, copies):
    return pl.pallas_call(
        kernel,
        out_shape=pltpu.VMEM(shape, source.dtype),
        in_specs=[HBM],
        out_specs=VMEM,
        scratch_shapes=[pltpu.SemaphoreType.DMA((copies,))],
        compiler_params=pltpu.CompilerParams(vmem_limit_bytes=2 * MIB),
        cost_estimate=pl.CostEstimate(
            flops=0, bytes_accessed=4 * math.prod(shape), transcendentals=0
        ),
    )(*in_hbm(source))


def load_in(w_in, first, tiles):
    units = w_in.shape[0]
    kernel = functools.partial(load_in_kernel, first)
    loaded = load(kernel, w_in, (tiles, units, 2, LANES), tiles)
    return loaded.reshape(tiles, 2 * units, LANES)


def expert_kernel(exp_dev, experts, count, *refs):
    group_ref = refs[0]
    x_refs = refs[1 : 1 + count]
    low_ref, high_ref, wout_ref, send_ref, keep_ref, mixed, hidden = refs[1 + count :]
    lines = low_ref.shape[1]
    width = wout_ref.shape[1]
    per = lines // exp_dev
    rows = sum(ref.shape[0] for ref in x_refs)
    x = jnp.concatenate([ref[:, :width] for ref in x_refs], axis=0)
    tail = jnp.concatenate([ref[:, width:] for ref in x_refs], axis=0)
    contract_last = (((1,), (1,)), ((), ()))
    column = lax.broadcasted_iota(jnp.int32, (16, tail.shape[1]), 1)
    wanted = lax.broadcasted_iota(jnp.int32, (16, tail.shape[1]), 0) + group_ref[0] * exp_dev
    select = (column % experts == wanted) & (column < 3 * experts)
    scale = lax.dot_general(
        select.astype(jnp.bfloat16), tail, contract_last, preferred_element_type=jnp.float32
    )
    for e in range(exp_dev):
        w = jnp.concatenate(
            [
                ref[t, pl.ds(e * per, per), :]
                for ref in (low_ref, high_ref)
                for t in range(ref.shape[0])
            ],
            axis=1,
        )
        both = lax.dot_general(w, x, contract_last, preferred_element_type=jnp.float32)
        for r in range(0, rows, LANES):
            mixed[...] = both[:, r : r + LANES]
            gate = mixed[pl.ds(0, per // 2, stride=2), :]
            up = mixed[pl.ds(1, per // 2, stride=2), :]
            act = gate / (1.0 + jnp.exp(-gate)) * up * scale[e : e + 1, r : r + LANES]
            hidden[pl.ds(e * per // 2, per // 2), r : r + LANES] = act.astype(jnp.bfloat16)
    chunk = min(512, width)
    pieces, piece, _ = keep_ref.shape
    for c in range(0, width, chunk):
        part = lax.dot_general(
            hidden[...],
            wout_ref[:, c : c + chunk],
            (((0,), (0,)), ((), ())),
            preferred_element_type=jnp.float32,
        )
        for p in range(pieces):
            keep_ref[p, :, c : c + chunk] = part[p * piece : (p + 1) * piece]
            other = part[(pieces + p) * piece : (pieces + p + 1) * piece]
            send_ref[p, :, c : c + chunk] = other.astype(jnp.bfloat16)


def run_experts(group, blocks, low, high, wout, exp_dev, experts):
    packed_width = blocks[0].shape[1]
    half_rows = sum(block.shape[0] for block in blocks) // 2
    count = len(blocks)
    width = wout.shape[1]
    lines = low.shape[1]
    one_step = half_rows <= LANES
    if one_step:
        x_block, out_block, grid = VMEM, VMEM, ()
        pieces, piece, rows = 1, half_rows, 2 * half_rows
        windows = 0
    else:
        pieces, piece, block = count // 2, blocks[0].shape[0], 16
        x_block = pl.BlockSpec((block, packed_width), lambda i: (i, 0))
        out_block = pl.BlockSpec((pieces, block, width), lambda i: (0, i, 0))
        grid = (piece // block,)
        rows = count * block
        windows = 2 * rows * (2 * packed_width + 3 * width)
    scratch = rows * (6 * lines + 6 * width)
    send, keep = pl.pallas_call(
        functools.partial(expert_kernel, exp_dev, experts, count),
        grid=grid,
        out_shape=(
            jax.ShapeDtypeStruct((pieces, piece, width), jnp.bfloat16),
            jax.ShapeDtypeStruct((pieces, piece, width), jnp.float32),
        ),
        in_specs=[pl.BlockSpec(memory_space=pltpu.SMEM), *[x_block] * count, VMEM, VMEM, VMEM],
        out_specs=[out_block, out_block],
        scratch_shapes=[
            pltpu.VMEM((lines // exp_dev, LANES), jnp.float32),
            pltpu.VMEM((lines // 2, rows), jnp.bfloat16),
        ],
        compiler_params=pltpu.CompilerParams(vmem_limit_bytes=windows + scratch + 4 * MIB),
        cost_estimate=pl.CostEstimate(
            flops=6 * half_rows * width * lines,
            bytes_accessed=4 * half_rows * packed_width + 6 * half_rows * width,
            transcendentals=half_rows * lines,
        ),
    )(group, *blocks, *in_vmem(low, high, wout))
    return send.reshape(half_rows, width), keep.reshape(half_rows, width)


def halve(rows, stride):
    size = rows.shape[0] // 2
    sent = rows[size:].astype(jnp.bfloat16)
    return rows[:size] + swap(sent, "expert", stride).astype(jnp.float32)


def body(tokens, expert_ids, route_weights, in_weights, out_weights):
    width = tokens.shape[1]
    exp_dev, units = in_weights.shape[:2]
    groups = lax.axis_size("expert")
    planes = lax.axis_size("batch")
    experts = exp_dev * groups
    far = planes - 1
    strides = [groups >> i for i in range(1, groups.bit_length() - 1)]
    w_in = in_weights.reshape(exp_dev * units, 2, width)
    w_out = out_weights.reshape(exp_dev * units, width)

    group = lax.axis_index("expert").astype(jnp.int32).reshape(1)
    x = pack(tokens, expert_ids, route_weights, experts)
    x, group, w_in, w_out = lax.optimization_barrier((x, group, w_in, w_out))
    tiles = width // LANES
    wout = load(load_out_kernel, w_out, w_out.shape, 8)
    for stride in strides[:-1]:
        x, wout = stack(x, swap(x, "expert", stride), [wout])
    x, w_in = lax.optimization_barrier((x, w_in))
    across = swap(x, "batch", far)
    mine = swap(x, "expert", strides[-1])
    low = load_in(w_in, 0, tiles // 2)
    across, mine, low = lax.optimization_barrier((across, mine, low))
    mine, wout, low = stack(x, mine, [wout, low])
    mine, across, w_in = lax.optimization_barrier((mine, across, w_in))
    early = [mine, across]
    late = [swap(mine, "batch", b) for b in range(1, far)]
    late.append(swap(across, "expert", strides[-1]))
    early_core = [swap(block, "expert", 1) for block in early]
    high = load_in(w_in, tiles // 2, tiles - tiles // 2)
    late, high = lax.optimization_barrier((late, high))
    late_core = [swap(block, "expert", 1) for block in late]
    blocks = []
    for (mine, across), rest in ((early, late), (early_core, late_core)):
        if 2 * mine.shape[0] * planes <= 2 * LANES:
            blocks += [mine] + rest[:-1] + [across, rest[-1]]
        else:
            blocks += [mine] + rest[:-1] + [jnp.concatenate([across, rest[-1]], axis=0)]

    send, total = run_experts(group, blocks, low, high, wout, exp_dev, experts)
    total = total + swap(send, "expert", 1).astype(jnp.float32)
    size = total.shape[0] // planes
    half = size // 2
    rounded = total.astype(jnp.bfloat16)
    starts = [b * size for b in range(1, far)]
    onward = [
        swap(rounded[start + half : start + size], "batch", b)
        for b, start in zip(range(1, far), starts)
    ]
    across = halve(total[far * size :], strides[-1])
    onward, staying = lax.optimization_barrier(
        (onward, [rounded[start : start + half] for start in starts])
    )
    sent = total[half:size]
    for rows in onward:
        sent = sent + rows.astype(jnp.float32)
    mine = total[:half]
    for b, rows in zip(range(1, far), staying):
        mine = mine + swap(rows, "batch", b).astype(jnp.float32)
    mine = mine + swap(sent.astype(jnp.bfloat16), "expert", strides[-1]).astype(jnp.float32)
    for stride in reversed(strides[:-1]):
        across = halve(across, stride)
    across = swap(across.astype(jnp.bfloat16), "batch", far).astype(jnp.float32)
    for stride in reversed(strides[:-1]):
        mine = halve(mine, stride)
    mine = mine + across
    return mine.astype(jnp.bfloat16)


def solution(mesh):
    return jax.shard_map(
        body,
        mesh=mesh,
        in_specs=(
            P(("batch", "expert"), None),
            P(("batch", "expert"), None),
            P(("batch", "expert"), None),
            P("expert", "batch", None, None),
            P("expert", "batch", None),
        ),
        out_specs=P(("batch", "expert"), None),
        check_vma=False,
    )
```

```python
import functools
import math

import jax
import jax.numpy as jnp
from jax import lax
from jax.experimental import pallas as pl
from jax.experimental.pallas import tpu as pltpu
from jax.sharding import PartitionSpec as P

LANES = 128
MIB = 1 << 20
VMEM = pl.BlockSpec(memory_space=pltpu.VMEM)
HBM = pl.BlockSpec(memory_space=pltpu.HBM)


def in_hbm(*arrays):
    return [pltpu.with_memory_space_constraint(array, pltpu.HBM) for array in arrays]


def in_vmem(*arrays):
    return [pltpu.with_memory_space_constraint(array, pltpu.VMEM) for array in arrays]


def swap(block, axis, flips):
    size = lax.axis_size(axis)
    return lax.ppermute(block, axis, [(i, i ^ flips) for i in range(size)])


def pack_kernel(
    experts, tokens_hbm, ids_hbm, weights_hbm, packed_ref, tokens_ref, ids_ref, weights_ref, sems
):
    copies = [
        pltpu.make_async_copy(source, target, sems.at[i])
        for i, (source, target) in enumerate(
            ((ids_hbm, ids_ref), (weights_hbm, weights_ref), (tokens_hbm, tokens_ref))
        )
    ]
    for copy in copies:
        copy.start()
    for copy in copies:
        copy.wait()
    rows, width = tokens_ref.shape
    tail = packed_ref.shape[1] - width
    packed_ref[:, :width] = tokens_ref[...]
    lane = lax.broadcasted_iota(jnp.int32, (rows, tail), 1)
    expert = lane % experts
    part = lane // experts
    dense = jnp.zeros((rows, tail), jnp.float32)
    for k in range(ids_ref.shape[1]):
        dense += jnp.where(ids_ref[:, k : k + 1] == expert, weights_ref[:, k : k + 1], 0.0)
    result = jnp.zeros((rows, tail), jnp.float32)
    for step in range(3):
        rounded = dense.astype(jnp.bfloat16).astype(jnp.float32)
        result = jnp.where(part == step, rounded, result)
        dense = dense - rounded
    packed_ref[:, width:] = result.astype(jnp.bfloat16)


def pack(tokens, expert_ids, route_weights, experts):
    rows, width = tokens.shape
    tail = -(-3 * experts // LANES) * LANES
    return pl.pallas_call(
        functools.partial(pack_kernel, experts),
        out_shape=jax.ShapeDtypeStruct((rows, width + tail), jnp.bfloat16),
        in_specs=[HBM] * 3,
        out_specs=VMEM,
        scratch_shapes=[
            pltpu.VMEM(tokens.shape, tokens.dtype),
            pltpu.VMEM(expert_ids.shape, expert_ids.dtype),
            pltpu.VMEM(route_weights.shape, route_weights.dtype),
            pltpu.SemaphoreType.DMA((3,)),
        ],
        compiler_params=pltpu.CompilerParams(vmem_limit_bytes=2 * MIB),
    )(*in_hbm(tokens, expert_ids, route_weights))


def stack_kernel(count, first_ref, second_ref, *refs):
    out_ref = refs[count]
    rows = first_ref.shape[0]
    out_ref[:rows, :] = first_ref[...]
    out_ref[rows:, :] = second_ref[...]


def stack(first, second, held):
    rows, width = first.shape
    return pl.pallas_call(
        functools.partial(stack_kernel, len(held)),
        out_shape=[jax.ShapeDtypeStruct((rows + second.shape[0], width), first.dtype)]
        + [pltpu.VMEM(array.shape, array.dtype) for array in held],
        in_specs=[VMEM] * (2 + len(held)),
        out_specs=[VMEM] * (1 + len(held)),
        input_output_aliases={2 + i: 1 + i for i in range(len(held))},
        compiler_params=pltpu.CompilerParams(vmem_limit_bytes=2 * MIB),
    )(first, second, *in_vmem(*held))


def load_in_kernel(first, in_ref, in_vmem, sems):
    copies = [
        pltpu.make_async_copy(
            in_ref.at[:, :, pl.ds((first + t) * LANES, LANES)], in_vmem.at[t], sems.at[t]
        )
        for t in range(in_vmem.shape[0])
    ]
    for copy in copies:
        copy.start()
    for copy in copies:
        copy.wait()


def load_out_kernel(out_ref, out_vmem, sems):
    copies = []
    step = out_ref.shape[0] // sems.shape[0]
    for i in range(sems.shape[0]):
        rows = pl.ds(i * step, step)
        copies.append(pltpu.make_async_copy(out_ref.at[rows], out_vmem.at[rows], sems.at[i]))
    for copy in copies:
        copy.start()
    for copy in copies:
        copy.wait()


def load(kernel, source, shape, copies):
    return pl.pallas_call(
        kernel,
        out_shape=pltpu.VMEM(shape, source.dtype),
        in_specs=[HBM],
        out_specs=VMEM,
        scratch_shapes=[pltpu.SemaphoreType.DMA((copies,))],
        compiler_params=pltpu.CompilerParams(vmem_limit_bytes=2 * MIB),
        cost_estimate=pl.CostEstimate(
            flops=0, bytes_accessed=4 * math.prod(shape), transcendentals=0
        ),
    )(*in_hbm(source))


def load_in(w_in, first, tiles):
    units = w_in.shape[0]
    kernel = functools.partial(load_in_kernel, first)
    loaded = load(kernel, w_in, (tiles, units, 2, LANES), tiles)
    return loaded.reshape(tiles, 2 * units, LANES)


def expert_kernel(exp_dev, experts, count, *refs):
    group_ref = refs[0]
    x_refs = refs[1 : 1 + count]
    low_ref, high_ref, wout_ref = refs[1 + count : 4 + count]
    send_refs, keep_refs = refs[4 + count : 6 + count], refs[6 + count : 8 + count]
    mixed, hidden = refs[8 + count :]
    lines = low_ref.shape[1]
    width = wout_ref.shape[1]
    per = lines // exp_dev
    rows = sum(ref.shape[0] for ref in x_refs)
    x = jnp.concatenate([ref[:, :width] for ref in x_refs], axis=0)
    tail = jnp.concatenate([ref[:, width:] for ref in x_refs], axis=0)
    contract_last = (((1,), (1,)), ((), ()))
    column = lax.broadcasted_iota(jnp.int32, (16, tail.shape[1]), 1)
    wanted = lax.broadcasted_iota(jnp.int32, (16, tail.shape[1]), 0) + group_ref[0] * exp_dev
    select = (column % experts == wanted) & (column < 3 * experts)
    scale = lax.dot_general(
        select.astype(jnp.bfloat16), tail, contract_last, preferred_element_type=jnp.float32
    )
    for e in range(exp_dev):
        w = jnp.concatenate(
            [
                ref[t, pl.ds(e * per, per), :]
                for ref in (low_ref, high_ref)
                for t in range(ref.shape[0])
            ],
            axis=1,
        )
        both = lax.dot_general(w, x, contract_last, preferred_element_type=jnp.float32)
        for r in range(0, rows, LANES):
            mixed[...] = both[:, r : r + LANES]
            gate = mixed[pl.ds(0, per // 2, stride=2), :]
            up = mixed[pl.ds(1, per // 2, stride=2), :]
            act = gate / (1.0 + jnp.exp(-gate)) * up * scale[e : e + 1, r : r + LANES]
            hidden[pl.ds(e * per // 2, per // 2), r : r + LANES] = act.astype(jnp.bfloat16)
    chunk = min(512, width)
    ahead, piece, _ = keep_refs[0].shape
    pieces = ahead + keep_refs[1].shape[0]
    for c in range(0, width, chunk):
        part = lax.dot_general(
            hidden[...],
            wout_ref[:, c : c + chunk],
            (((0,), (0,)), ((), ())),
            preferred_element_type=jnp.float32,
        )
        for p in range(2 * pieces):
            targets = keep_refs if p < pieces else send_refs
            q = p % pieces
            target = targets[0].at[q] if q < ahead else targets[1].at[q - ahead]
            target[:, c : c + chunk] = part[p * piece : (p + 1) * piece].astype(target.dtype)


def run_experts(group, blocks, pieces, low, high, wout, exp_dev, experts):
    packed_width = blocks[0].shape[1]
    half_rows = sum(block.shape[0] for block in blocks) // 2
    piece = half_rows // pieces
    ahead, after = 1, pieces - 1
    count = len(blocks)
    width = wout.shape[1]
    lines = low.shape[1]
    if half_rows <= LANES:
        x_block, out_blocks, grid = VMEM, [VMEM] * 4, ()
        rows, windows = 2 * half_rows, 0
    else:
        block = 16
        x_block = pl.BlockSpec((block, packed_width), lambda i: (i, 0))
        out_blocks = [
            pl.BlockSpec((n, block, width), lambda i: (0, i, 0)) for n in (ahead, after) * 2
        ]
        grid = (piece // block,)
        rows = count * block
        windows = 2 * rows * (2 * packed_width + 3 * width)
    scratch = rows * (6 * lines + 6 * width)
    return pl.pallas_call(
        functools.partial(expert_kernel, exp_dev, experts, count),
        grid=grid,
        out_shape=(
            jax.ShapeDtypeStruct((ahead, piece, width), jnp.bfloat16),
            jax.ShapeDtypeStruct((after, piece, width), jnp.bfloat16),
            jax.ShapeDtypeStruct((ahead, piece, width), jnp.float32),
            jax.ShapeDtypeStruct((after, piece, width), jnp.float32),
        ),
        in_specs=[pl.BlockSpec(memory_space=pltpu.SMEM), *[x_block] * count, VMEM, VMEM, VMEM],
        out_specs=out_blocks,
        scratch_shapes=[
            pltpu.VMEM((lines // exp_dev, LANES), jnp.float32),
            pltpu.VMEM((lines // 2, rows), jnp.bfloat16),
        ],
        compiler_params=pltpu.CompilerParams(vmem_limit_bytes=windows + scratch + 4 * MIB),
        cost_estimate=pl.CostEstimate(
            flops=6 * half_rows * width * lines,
            bytes_accessed=4 * half_rows * packed_width + 6 * half_rows * width,
            transcendentals=half_rows * lines,
        ),
    )(group, *blocks, *in_vmem(low, high, wout))


def halve(rows, stride):
    size = rows.shape[0] // 2
    sent = rows[size:].astype(jnp.bfloat16)
    return rows[:size] + swap(sent, "expert", stride).astype(jnp.float32)


def body(tokens, expert_ids, route_weights, in_weights, out_weights):
    width = tokens.shape[1]
    exp_dev, units = in_weights.shape[:2]
    groups = lax.axis_size("expert")
    planes = lax.axis_size("batch")
    experts = exp_dev * groups
    far = planes - 1
    strides = [groups >> i for i in range(1, groups.bit_length() - 1)]
    w_in = in_weights.reshape(exp_dev * units, 2, width)
    w_out = out_weights.reshape(exp_dev * units, width)

    group = lax.axis_index("expert").astype(jnp.int32).reshape(1)
    x = pack(tokens, expert_ids, route_weights, experts)
    x, group, w_in, w_out = lax.optimization_barrier((x, group, w_in, w_out))
    tiles = width // LANES
    wout = load(load_out_kernel, w_out, w_out.shape, 8)
    for stride in strides[:-1]:
        x, wout = stack(x, swap(x, "expert", stride), [wout])
    x, w_in = lax.optimization_barrier((x, w_in))
    across = swap(x, "batch", far)
    mine = swap(x, "expert", strides[-1])
    low = load_in(w_in, 0, tiles // 2)
    across, mine, low = lax.optimization_barrier((across, mine, low))
    mine, wout, low = stack(x, mine, [wout, low])
    mine, across, w_in = lax.optimization_barrier((mine, across, w_in))
    early = [mine, across]
    late = [swap(mine, "batch", b) for b in range(1, far)]
    late.append(swap(across, "expert", strides[-1]))
    early_core = [swap(block, "expert", 1) for block in early]
    high = load_in(w_in, tiles // 2, tiles - tiles // 2)
    late, high = lax.optimization_barrier((late, high))
    late_core = [swap(block, "expert", 1) for block in late]
    blocks = []
    for (mine, across), rest in ((early, late), (early_core, late_core)):
        if mine.shape[0] * planes <= LANES:
            blocks += [across, rest[-1], mine] + rest[:-1]
        else:
            blocks += [jnp.concatenate([across, rest[-1]], axis=0), mine] + rest[:-1]

    sends = run_experts(group, blocks, planes, low, high, wout, exp_dev, experts)
    first, second, across, total = sends
    across = across[0] + swap(first, "expert", 1)[0].astype(jnp.float32)
    total = total + swap(second, "expert", 1).astype(jnp.float32)
    half = total.shape[1] // 2
    rounded = total.astype(jnp.bfloat16)
    onward = [swap(rounded[b, half:], "batch", b) for b in range(1, far)]
    across = halve(across, strides[-1])
    onward, staying = lax.optimization_barrier(
        (onward, [rounded[b, :half] for b in range(1, far)])
    )
    sent = total[0, half:]
    for rows in onward:
        sent = sent + rows.astype(jnp.float32)
    mine = total[0, :half]
    for b, rows in zip(range(1, far), staying):
        mine = mine + swap(rows, "batch", b).astype(jnp.float32)
    mine = mine + swap(sent.astype(jnp.bfloat16), "expert", strides[-1]).astype(jnp.float32)
    for stride in reversed(strides[:-1]):
        across = halve(across, stride)
    across = swap(across.astype(jnp.bfloat16), "batch", far).astype(jnp.float32)
    for stride in reversed(strides[:-1]):
        mine = halve(mine, stride)
    mine = mine + across
    return mine.astype(jnp.bfloat16)


def solution(mesh):
    return jax.shard_map(
        body,
        mesh=mesh,
        in_specs=(
            P(("batch", "expert"), None),
            P(("batch", "expert"), None),
            P(("batch", "expert"), None),
            P("expert", "batch", None, None),
            P("expert", "batch", None),
        ),
        out_specs=P(("batch", "expert"), None),
        check_vma=False,
    )
```

```python
import functools
import math

import jax
import jax.numpy as jnp
from jax import lax
from jax.experimental import pallas as pl
from jax.experimental.pallas import tpu as pltpu
from jax.sharding import PartitionSpec as P

LANES = 128
MIB = 1 << 20
VMEM = pl.BlockSpec(memory_space=pltpu.VMEM)
HBM = pl.BlockSpec(memory_space=pltpu.HBM)


def in_hbm(*arrays):
    return [pltpu.with_memory_space_constraint(array, pltpu.HBM) for array in arrays]


def in_vmem(*arrays):
    return [pltpu.with_memory_space_constraint(array, pltpu.VMEM) for array in arrays]


def swap(block, axis, flips):
    size = lax.axis_size(axis)
    return lax.ppermute(block, axis, [(i, i ^ flips) for i in range(size)])


def pack_kernel(
    experts, tokens_hbm, ids_hbm, weights_hbm, packed_ref, tokens_ref, ids_ref, weights_ref, sems
):
    copies = [
        pltpu.make_async_copy(source, target, sems.at[i])
        for i, (source, target) in enumerate(
            ((ids_hbm, ids_ref), (weights_hbm, weights_ref), (tokens_hbm, tokens_ref))
        )
    ]
    for copy in copies:
        copy.start()
    for copy in copies:
        copy.wait()
    rows, width = tokens_ref.shape
    tail = packed_ref.shape[1] - width
    packed_ref[:, :width] = tokens_ref[...]
    lane = lax.broadcasted_iota(jnp.int32, (rows, tail), 1)
    expert = lane % experts
    part = lane // experts
    dense = jnp.zeros((rows, tail), jnp.float32)
    for k in range(ids_ref.shape[1]):
        dense += jnp.where(ids_ref[:, k : k + 1] == expert, weights_ref[:, k : k + 1], 0.0)
    result = jnp.zeros((rows, tail), jnp.float32)
    for step in range(3):
        rounded = dense.astype(jnp.bfloat16).astype(jnp.float32)
        result = jnp.where(part == step, rounded, result)
        dense = dense - rounded
    packed_ref[:, width:] = result.astype(jnp.bfloat16)


def pack(tokens, expert_ids, route_weights, experts):
    rows, width = tokens.shape
    tail = -(-3 * experts // LANES) * LANES
    return pl.pallas_call(
        functools.partial(pack_kernel, experts),
        out_shape=jax.ShapeDtypeStruct((rows, width + tail), jnp.bfloat16),
        in_specs=[HBM] * 3,
        out_specs=VMEM,
        scratch_shapes=[
            pltpu.VMEM(tokens.shape, tokens.dtype),
            pltpu.VMEM(expert_ids.shape, expert_ids.dtype),
            pltpu.VMEM(route_weights.shape, route_weights.dtype),
            pltpu.SemaphoreType.DMA((3,)),
        ],
        compiler_params=pltpu.CompilerParams(vmem_limit_bytes=2 * MIB),
    )(*in_hbm(tokens, expert_ids, route_weights))


def stack_kernel(count, first_ref, second_ref, *refs):
    out_ref = refs[count]
    rows = first_ref.shape[0]
    out_ref[:rows, :] = first_ref[...]
    out_ref[rows:, :] = second_ref[...]


def stack(first, second, held):
    rows, width = first.shape
    return pl.pallas_call(
        functools.partial(stack_kernel, len(held)),
        out_shape=[jax.ShapeDtypeStruct((rows + second.shape[0], width), first.dtype)]
        + [pltpu.VMEM(array.shape, array.dtype) for array in held],
        in_specs=[VMEM] * (2 + len(held)),
        out_specs=[VMEM] * (1 + len(held)),
        input_output_aliases={2 + i: 1 + i for i in range(len(held))},
        compiler_params=pltpu.CompilerParams(vmem_limit_bytes=2 * MIB),
    )(first, second, *in_vmem(*held))


def load_in_kernel(first, in_ref, in_vmem, sems):
    copies = [
        pltpu.make_async_copy(
            in_ref.at[:, :, pl.ds((first + t) * LANES, LANES)], in_vmem.at[t], sems.at[t]
        )
        for t in range(in_vmem.shape[0])
    ]
    for copy in copies:
        copy.start()
    for copy in copies:
        copy.wait()


def load_out_kernel(out_ref, out_vmem, sems):
    copies = []
    step = out_ref.shape[0] // sems.shape[0]
    for i in range(sems.shape[0]):
        rows = pl.ds(i * step, step)
        copies.append(pltpu.make_async_copy(out_ref.at[rows], out_vmem.at[rows], sems.at[i]))
    for copy in copies:
        copy.start()
    for copy in copies:
        copy.wait()


def load(kernel, source, shape, copies):
    return pl.pallas_call(
        kernel,
        out_shape=pltpu.VMEM(shape, source.dtype),
        in_specs=[HBM],
        out_specs=VMEM,
        scratch_shapes=[pltpu.SemaphoreType.DMA((copies,))],
        compiler_params=pltpu.CompilerParams(vmem_limit_bytes=2 * MIB),
        cost_estimate=pl.CostEstimate(
            flops=0, bytes_accessed=4 * math.prod(shape), transcendentals=0
        ),
    )(*in_hbm(source))


def load_in(w_in, first, tiles):
    units = w_in.shape[0]
    kernel = functools.partial(load_in_kernel, first)
    loaded = load(kernel, w_in, (tiles, units, 2, LANES), tiles)
    return loaded.reshape(tiles, 2 * units, LANES)


def expert_kernel(exp_dev, experts, count, *refs):
    group_ref = refs[0]
    x_refs = refs[1 : 1 + count]
    low_ref, high_ref, wout_ref, send_ref, keep_ref, mixed, hidden = refs[1 + count :]
    lines = low_ref.shape[1]
    width = wout_ref.shape[1]
    per = lines // exp_dev
    rows = sum(ref.shape[0] for ref in x_refs)
    x = jnp.concatenate([ref[:, :width] for ref in x_refs], axis=0)
    tail = jnp.concatenate([ref[:, width:] for ref in x_refs], axis=0)
    contract_last = (((1,), (1,)), ((), ()))
    column = lax.broadcasted_iota(jnp.int32, (16, tail.shape[1]), 1)
    wanted = lax.broadcasted_iota(jnp.int32, (16, tail.shape[1]), 0) + group_ref[0] * exp_dev
    select = (column % experts == wanted) & (column < 3 * experts)
    scale = lax.dot_general(
        select.astype(jnp.bfloat16), tail, contract_last, preferred_element_type=jnp.float32
    )
    for e in range(exp_dev):
        w = jnp.concatenate(
            [
                ref[t, pl.ds(e * per, per), :]
                for ref in (low_ref, high_ref)
                for t in range(ref.shape[0])
            ],
            axis=1,
        )
        both = lax.dot_general(w, x, contract_last, preferred_element_type=jnp.float32)
        for r in range(0, rows, LANES):
            mixed[...] = both[:, r : r + LANES]
            gate = mixed[pl.ds(0, per // 2, stride=2), :]
            up = mixed[pl.ds(1, per // 2, stride=2), :]
            act = gate / (1.0 + jnp.exp(-gate)) * up * scale[e : e + 1, r : r + LANES]
            hidden[pl.ds(e * per // 2, per // 2), r : r + LANES] = act.astype(jnp.bfloat16)
    chunk = min(512, width)
    pieces, piece, _ = keep_ref.shape
    for c in range(0, width, chunk):
        part = lax.dot_general(
            hidden[...],
            wout_ref[:, c : c + chunk],
            (((0,), (0,)), ((), ())),
            preferred_element_type=jnp.float32,
        )
        for p in range(pieces):
            keep_ref[p, :, c : c + chunk] = part[p * piece : (p + 1) * piece]
            other = part[(pieces + p) * piece : (pieces + p + 1) * piece]
            send_ref[p, :, c : c + chunk] = other.astype(jnp.bfloat16)


def run_experts(group, blocks, low, high, wout, exp_dev, experts):
    packed_width = blocks[0].shape[1]
    half_rows = sum(block.shape[0] for block in blocks) // 2
    count = len(blocks)
    width = wout.shape[1]
    lines = low.shape[1]
    one_step = half_rows <= LANES
    if one_step:
        x_block, out_block, grid = VMEM, VMEM, ()
        pieces, piece, rows = 1, half_rows, 2 * half_rows
        windows = 0
    else:
        pieces, piece, block = count // 2, blocks[0].shape[0], 16
        x_block = pl.BlockSpec((block, packed_width), lambda i: (i, 0))
        out_block = pl.BlockSpec((pieces, block, width), lambda i: (0, i, 0))
        grid = (piece // block,)
        rows = count * block
        windows = 2 * rows * (2 * packed_width + 3 * width)
    scratch = rows * (6 * lines + 6 * width)
    send, keep = pl.pallas_call(
        functools.partial(expert_kernel, exp_dev, experts, count),
        grid=grid,
        out_shape=(
            jax.ShapeDtypeStruct((pieces, piece, width), jnp.bfloat16),
            jax.ShapeDtypeStruct((pieces, piece, width), jnp.float32),
        ),
        in_specs=[pl.BlockSpec(memory_space=pltpu.SMEM), *[x_block] * count, VMEM, VMEM, VMEM],
        out_specs=[out_block, out_block],
        scratch_shapes=[
            pltpu.VMEM((lines // exp_dev, LANES), jnp.float32),
            pltpu.VMEM((lines // 2, rows), jnp.bfloat16),
        ],
        compiler_params=pltpu.CompilerParams(vmem_limit_bytes=windows + scratch + 4 * MIB),
        cost_estimate=pl.CostEstimate(
            flops=6 * half_rows * width * lines,
            bytes_accessed=4 * half_rows * packed_width + 6 * half_rows * width,
            transcendentals=half_rows * lines,
        ),
    )(group, *blocks, *in_vmem(low, high, wout))
    return send.reshape(half_rows, width), keep.reshape(half_rows, width)


def halve(rows, stride):
    size = rows.shape[0] // 2
    sent = rows[size:].astype(jnp.bfloat16)
    return rows[:size] + swap(sent, "expert", stride).astype(jnp.float32)


def body(tokens, expert_ids, route_weights, in_weights, out_weights):
    width = tokens.shape[1]
    exp_dev, units = in_weights.shape[:2]
    groups = lax.axis_size("expert")
    planes = lax.axis_size("batch")
    experts = exp_dev * groups
    far = planes - 1
    strides = [groups >> i for i in range(1, groups.bit_length() - 1)]
    w_in = in_weights.reshape(exp_dev * units, 2, width)
    w_out = out_weights.reshape(exp_dev * units, width)

    group = lax.axis_index("expert").astype(jnp.int32).reshape(1)
    x = pack(tokens, expert_ids, route_weights, experts)
    x, group, w_in, w_out = lax.optimization_barrier((x, group, w_in, w_out))
    tiles = width // LANES
    wout = load(load_out_kernel, w_out, w_out.shape, 8)
    for stride in strides[:-1]:
        x, wout = stack(x, swap(x, "expert", stride), [wout])
    x, w_in = lax.optimization_barrier((x, w_in))
    across = swap(x, "batch", far)
    mine = swap(x, "expert", strides[-1])
    low = load_in(w_in, 0, tiles // 2)
    across, mine, low = lax.optimization_barrier((across, mine, low))
    mine, wout, low = stack(x, mine, [wout, low])
    mine, across, w_in = lax.optimization_barrier((mine, across, w_in))
    early = [mine, across]
    late = [swap(mine, "batch", b) for b in range(1, far)]
    late.append(swap(across, "expert", strides[-1]))
    early_core = [swap(block, "expert", 1) for block in early]
    high = load_in(w_in, tiles // 2, tiles - tiles // 2)
    late, high = lax.optimization_barrier((late, high))
    late_core = [swap(block, "expert", 1) for block in late]
    blocks = []
    for (mine, across), rest in ((early, late), (early_core, late_core)):
        if 2 * mine.shape[0] * planes <= 2 * LANES:
            blocks += [mine] + rest[:-1] + [across, rest[-1]]
        else:
            blocks += [mine] + rest[:-1] + [jnp.concatenate([across, rest[-1]], axis=0)]

    send, total = run_experts(group, blocks, low, high, wout, exp_dev, experts)
    total = total + swap(send, "expert", 1).astype(jnp.float32)
    total = total.reshape(planes, -1, width)
    half = total.shape[1] // 2
    rounded = total.astype(jnp.bfloat16)
    across = halve(total[far], strides[-1])
    onward = [swap(rounded[b, half:], "batch", b) for b in range(1, far)]
    own = tokens.shape[0]
    onward, middle = lax.optimization_barrier(
        (onward, [rounded[b, own:half] for b in range(1, far)])
    )
    sent = total[0, half:]
    for rows in onward:
        sent = sent + rows.astype(jnp.float32)
    middle = [swap(rows, "batch", b) for b, rows in zip(range(1, far), middle)]
    middle, last = lax.optimization_barrier(
        (middle, [rounded[b, :own] for b in range(1, far)])
    )
    arrived = swap(sent.astype(jnp.bfloat16), "expert", strides[-1]).astype(jnp.float32)
    mine = total[0, :own] + arrived[:own]
    rest = total[0, own:half] + arrived[own:]
    for rows in middle:
        rest = rest + rows.astype(jnp.float32)
    for stride in reversed(strides[:-1]):
        across = halve(across, stride)
    across = swap(across.astype(jnp.bfloat16), "batch", far).astype(jnp.float32)
    size = half
    for stride in reversed(strides[:-1]):
        size = size // 2
        sent = rest[size - own :].astype(jnp.bfloat16)
        arrived = swap(sent, "expert", stride).astype(jnp.float32)
        mine = mine + arrived[:own]
        if size > own:
            rest = rest[: size - own] + arrived[own:]
    for b, rows in zip(range(1, far), last):
        mine = mine + swap(rows, "batch", b).astype(jnp.float32)
    mine = mine + across
    return mine.astype(jnp.bfloat16)


def solution(mesh):
    return jax.shard_map(
        body,
        mesh=mesh,
        in_specs=(
            P(("batch", "expert"), None),
            P(("batch", "expert"), None),
            P(("batch", "expert"), None),
            P("expert", "batch", None, None),
            P("expert", "batch", None),
        ),
        out_specs=P(("batch", "expert"), None),
        check_vma=False,
    )
```

```python
import functools
import math

import jax
import jax.numpy as jnp
from jax import lax
from jax.experimental import pallas as pl
from jax.experimental.pallas import tpu as pltpu
from jax.sharding import PartitionSpec as P

LANES = 128
MIB = 1 << 20
VMEM = pl.BlockSpec(memory_space=pltpu.VMEM)
HBM = pl.BlockSpec(memory_space=pltpu.HBM)


def in_hbm(*arrays):
    return [pltpu.with_memory_space_constraint(array, pltpu.HBM) for array in arrays]


def in_vmem(*arrays):
    return [pltpu.with_memory_space_constraint(array, pltpu.VMEM) for array in arrays]


def swap(block, axis, flips):
    size = lax.axis_size(axis)
    return lax.ppermute(block, axis, [(i, i ^ flips) for i in range(size)])


def pack_kernel(
    experts, tokens_hbm, ids_hbm, weights_hbm, packed_ref, tokens_ref, ids_ref, weights_ref, sems
):
    copies = [
        pltpu.make_async_copy(source, target, sems.at[i])
        for i, (source, target) in enumerate(
            ((ids_hbm, ids_ref), (weights_hbm, weights_ref), (tokens_hbm, tokens_ref))
        )
    ]
    for copy in copies:
        copy.start()
    for copy in copies:
        copy.wait()
    rows, width = tokens_ref.shape
    tail = packed_ref.shape[1] - width
    packed_ref[:, :width] = tokens_ref[...]
    lane = lax.broadcasted_iota(jnp.int32, (rows, tail), 1)
    expert = lane % experts
    part = lane // experts
    dense = jnp.zeros((rows, tail), jnp.float32)
    for k in range(ids_ref.shape[1]):
        dense += jnp.where(ids_ref[:, k : k + 1] == expert, weights_ref[:, k : k + 1], 0.0)
    result = jnp.zeros((rows, tail), jnp.float32)
    for step in range(3):
        rounded = dense.astype(jnp.bfloat16).astype(jnp.float32)
        result = jnp.where(part == step, rounded, result)
        dense = dense - rounded
    packed_ref[:, width:] = result.astype(jnp.bfloat16)


def pack(tokens, expert_ids, route_weights, experts):
    rows, width = tokens.shape
    tail = -(-3 * experts // LANES) * LANES
    return pl.pallas_call(
        functools.partial(pack_kernel, experts),
        out_shape=jax.ShapeDtypeStruct((rows, width + tail), jnp.bfloat16),
        in_specs=[HBM] * 3,
        out_specs=VMEM,
        scratch_shapes=[
            pltpu.VMEM(tokens.shape, tokens.dtype),
            pltpu.VMEM(expert_ids.shape, expert_ids.dtype),
            pltpu.VMEM(route_weights.shape, route_weights.dtype),
            pltpu.SemaphoreType.DMA((3,)),
        ],
        compiler_params=pltpu.CompilerParams(vmem_limit_bytes=2 * MIB),
    )(*in_hbm(tokens, expert_ids, route_weights))


def stack_kernel(count, first_ref, second_ref, *refs):
    out_ref = refs[count]
    rows = first_ref.shape[0]
    out_ref[:rows, :] = first_ref[...]
    out_ref[rows:, :] = second_ref[...]


def stack(first, second, held):
    rows, width = first.shape
    return pl.pallas_call(
        functools.partial(stack_kernel, len(held)),
        out_shape=[jax.ShapeDtypeStruct((rows + second.shape[0], width), first.dtype)]
        + [pltpu.VMEM(array.shape, array.dtype) for array in held],
        in_specs=[VMEM] * (2 + len(held)),
        out_specs=[VMEM] * (1 + len(held)),
        input_output_aliases={2 + i: 1 + i for i in range(len(held))},
        compiler_params=pltpu.CompilerParams(vmem_limit_bytes=2 * MIB),
    )(first, second, *in_vmem(*held))


def load_in_kernel(first, in_ref, in_vmem, sems):
    copies = [
        pltpu.make_async_copy(
            in_ref.at[:, :, pl.ds((first + t) * LANES, LANES)], in_vmem.at[t], sems.at[t]
        )
        for t in range(in_vmem.shape[0])
    ]
    for copy in copies:
        copy.start()
    for copy in copies:
        copy.wait()


def load_out_kernel(out_ref, out_vmem, sems):
    copies = []
    step = out_ref.shape[0] // sems.shape[0]
    for i in range(sems.shape[0]):
        rows = pl.ds(i * step, step)
        copies.append(pltpu.make_async_copy(out_ref.at[rows], out_vmem.at[rows], sems.at[i]))
    for copy in copies:
        copy.start()
    for copy in copies:
        copy.wait()


def load(kernel, source, shape, copies):
    return pl.pallas_call(
        kernel,
        out_shape=pltpu.VMEM(shape, source.dtype),
        in_specs=[HBM],
        out_specs=VMEM,
        scratch_shapes=[pltpu.SemaphoreType.DMA((copies,))],
        compiler_params=pltpu.CompilerParams(vmem_limit_bytes=2 * MIB),
        cost_estimate=pl.CostEstimate(
            flops=0, bytes_accessed=4 * math.prod(shape), transcendentals=0
        ),
    )(*in_hbm(source))


def load_in(w_in, first, tiles):
    units = w_in.shape[0]
    kernel = functools.partial(load_in_kernel, first)
    loaded = load(kernel, w_in, (tiles, units, 2, LANES), tiles)
    return loaded.reshape(tiles, 2 * units, LANES)


def expert_kernel(exp_dev, experts, count, *refs):
    group_ref = refs[0]
    x_refs = refs[1 : 1 + count]
    low_ref, high_ref, wout_ref = refs[1 + count : 4 + count]
    send_refs, keep_refs = refs[4 + count : 6 + count], refs[6 + count : 8 + count]
    mixed, hidden = refs[8 + count :]
    lines = low_ref.shape[1]
    width = wout_ref.shape[1]
    per = lines // exp_dev
    rows = sum(ref.shape[0] for ref in x_refs)
    x = jnp.concatenate([ref[:, :width] for ref in x_refs], axis=0)
    tail = jnp.concatenate([ref[:, width:] for ref in x_refs], axis=0)
    contract_last = (((1,), (1,)), ((), ()))
    column = lax.broadcasted_iota(jnp.int32, (16, tail.shape[1]), 1)
    wanted = lax.broadcasted_iota(jnp.int32, (16, tail.shape[1]), 0) + group_ref[0] * exp_dev
    select = (column % experts == wanted) & (column < 3 * experts)
    scale = lax.dot_general(
        select.astype(jnp.bfloat16), tail, contract_last, preferred_element_type=jnp.float32
    )
    for e in range(exp_dev):
        w = jnp.concatenate(
            [
                ref[t, pl.ds(e * per, per), :]
                for ref in (low_ref, high_ref)
                for t in range(ref.shape[0])
            ],
            axis=1,
        )
        both = lax.dot_general(w, x, contract_last, preferred_element_type=jnp.float32)
        for r in range(0, rows, LANES):
            mixed[...] = both[:, r : r + LANES]
            gate = mixed[pl.ds(0, per // 2, stride=2), :]
            up = mixed[pl.ds(1, per // 2, stride=2), :]
            act = gate / (1.0 + jnp.exp(-gate)) * up * scale[e : e + 1, r : r + LANES]
            hidden[pl.ds(e * per // 2, per // 2), r : r + LANES] = act.astype(jnp.bfloat16)
    chunk = min(512, width)
    ahead, piece, _ = keep_refs[0].shape
    pieces = ahead + keep_refs[1].shape[0]
    by_row = hidden[...].T
    for c in range(0, width, chunk):
        part = jnp.dot(by_row, wout_ref[:, c : c + chunk], preferred_element_type=jnp.float32)
        for p in range(2 * pieces):
            targets = keep_refs if p < pieces else send_refs
            q = p % pieces
            target = targets[0].at[q] if q < ahead else targets[1].at[q - ahead]
            target[:, c : c + chunk] = part[p * piece : (p + 1) * piece].astype(target.dtype)


def run_experts(group, blocks, pieces, low, high, wout, exp_dev, experts):
    packed_width = blocks[0].shape[1]
    half_rows = sum(block.shape[0] for block in blocks) // 2
    piece = half_rows // pieces
    ahead, after = 1, pieces - 1
    count = len(blocks)
    width = wout.shape[1]
    lines = low.shape[1]
    if half_rows <= LANES:
        x_block, out_blocks, grid = VMEM, [VMEM] * 4, ()
        rows, windows = 2 * half_rows, 0
    else:
        block = 16
        x_block = pl.BlockSpec((block, packed_width), lambda i: (i, 0))
        out_blocks = [
            pl.BlockSpec((n, block, width), lambda i: (0, i, 0)) for n in (ahead, after) * 2
        ]
        grid = (piece // block,)
        rows = count * block
        windows = 2 * rows * (2 * packed_width + 3 * width)
    scratch = rows * (6 * lines + 6 * width)
    return pl.pallas_call(
        functools.partial(expert_kernel, exp_dev, experts, count),
        grid=grid,
        out_shape=(
            jax.ShapeDtypeStruct((ahead, piece, width), jnp.bfloat16),
            jax.ShapeDtypeStruct((after, piece, width), jnp.bfloat16),
            jax.ShapeDtypeStruct((ahead, piece, width), jnp.float32),
            jax.ShapeDtypeStruct((after, piece, width), jnp.float32),
        ),
        in_specs=[pl.BlockSpec(memory_space=pltpu.SMEM), *[x_block] * count, VMEM, VMEM, VMEM],
        out_specs=out_blocks,
        scratch_shapes=[
            pltpu.VMEM((lines // exp_dev, LANES), jnp.float32),
            pltpu.VMEM((lines // 2, rows), jnp.bfloat16),
        ],
        compiler_params=pltpu.CompilerParams(vmem_limit_bytes=windows + scratch + 4 * MIB),
        cost_estimate=pl.CostEstimate(
            flops=6 * half_rows * width * lines,
            bytes_accessed=4 * half_rows * packed_width + 6 * half_rows * width,
            transcendentals=half_rows * lines,
        ),
    )(group, *blocks, *in_vmem(low, high, wout))


def halve(rows, stride):
    size = rows.shape[0] // 2
    sent = rows[size:].astype(jnp.bfloat16)
    return rows[:size] + swap(sent, "expert", stride).astype(jnp.float32)


def body(tokens, expert_ids, route_weights, in_weights, out_weights):
    width = tokens.shape[1]
    exp_dev, units = in_weights.shape[:2]
    groups = lax.axis_size("expert")
    planes = lax.axis_size("batch")
    experts = exp_dev * groups
    far = planes - 1
    strides = [groups >> i for i in range(1, groups.bit_length() - 1)]
    w_in = in_weights.reshape(exp_dev * units, 2, width)
    w_out = out_weights.reshape(exp_dev * units, width)

    group = lax.axis_index("expert").astype(jnp.int32).reshape(1)
    x = pack(tokens, expert_ids, route_weights, experts)
    x, group, w_in, w_out = lax.optimization_barrier((x, group, w_in, w_out))
    tiles = width // LANES
    wout = load(load_out_kernel, w_out, w_out.shape, 8)
    for stride in strides[:-1]:
        x, wout = stack(x, swap(x, "expert", stride), [wout])
    x, w_in = lax.optimization_barrier((x, w_in))
    across = swap(x, "batch", far)
    mine = swap(x, "expert", strides[-1])
    low = load_in(w_in, 0, tiles // 2)
    across, mine, low = lax.optimization_barrier((across, mine, low))
    mine, wout, low = stack(x, mine, [wout, low])
    mine, across, w_in = lax.optimization_barrier((mine, across, w_in))
    early = [mine, across]
    late = [swap(mine, "batch", b) for b in range(1, far)]
    late.append(swap(across, "expert", strides[-1]))
    early_core = [swap(block, "expert", 1) for block in early]
    high = load_in(w_in, tiles // 2, tiles - tiles // 2)
    late, high = lax.optimization_barrier((late, high))
    late_core = [swap(block, "expert", 1) for block in late]
    blocks = []
    for (mine, across), rest in ((early, late), (early_core, late_core)):
        if mine.shape[0] * planes <= LANES:
            blocks += [across, rest[-1], mine] + rest[:-1]
        else:
            blocks += [jnp.concatenate([across, rest[-1]], axis=0), mine] + rest[:-1]

    sends = run_experts(group, blocks, planes, low, high, wout, exp_dev, experts)
    first, second, across, total = sends
    across = across[0] + swap(first, "expert", 1)[0].astype(jnp.float32)
    total = total + swap(second, "expert", 1).astype(jnp.float32)
    half = total.shape[1] // 2
    rounded = total.astype(jnp.bfloat16)
    onward = [swap(rounded[b, half:], "batch", b) for b in range(1, far)]
    across = halve(across, strides[-1])
    onward, staying = lax.optimization_barrier(
        (onward, [rounded[b, :half] for b in range(1, far)])
    )
    sent = total[0, half:]
    for rows in onward:
        sent = sent + rows.astype(jnp.float32)
    mine = total[0, :half]
    for b, rows in zip(range(1, far), staying):
        mine = mine + swap(rows, "batch", b).astype(jnp.float32)
    mine = mine + swap(sent.astype(jnp.bfloat16), "expert", strides[-1]).astype(jnp.float32)
    for stride in reversed(strides[:-1]):
        across = halve(across, stride)
    across = swap(across.astype(jnp.bfloat16), "batch", far).astype(jnp.float32)
    for stride in reversed(strides[:-1]):
        mine = halve(mine, stride)
    mine = mine + across
    return mine.astype(jnp.bfloat16)


def solution(mesh):
    return jax.shard_map(
        body,
        mesh=mesh,
        in_specs=(
            P(("batch", "expert"), None),
            P(("batch", "expert"), None),
            P(("batch", "expert"), None),
            P("expert", "batch", None, None),
            P("expert", "batch", None),
        ),
        out_specs=P(("batch", "expert"), None),
        check_vma=False,
    )
```
